512 devices in a mesh: il: 64 (over z_hi, y, core), xl: 8 (over z_lo, x).
Axes of the slice: x: 4, y: 8, z: 8 (z_hi: 4, z_lo: 2; z = z_hi * 2 + z_lo), core: 2. Of those that a mesh axis runs over, the one named last changes fastest.
Arguments:
- solution: float32 [256, 512, 512], P('il', 'xl'), may hold values from -6 to 6
- residual: float32 [256, 512, 512], P('il', 'xl'), may hold values from -30 to 30
- direction: float32 [256, 512, 512], P('il', 'xl'), may hold values from -30 to 30
- slope_il: float32 [256, 512, 512], P('il', 'xl'), may hold values from -1.5 to 1.5
- slope_xl: float32 [256, 512, 512], P('il', 'xl'), may hold values from -1.5 to 1.5
- weights: float32 [256, 512, 512], P('il', 'xl'), may hold values from 0.2 to 1
Outputs:
- new_solution: float32 [256, 512, 512], P('il', 'xl')
- new_residual: float32 [256, 512, 512], P('il', 'xl')
- new_direction: float32 [256, 512, 512], P('il', 'xl')
The draws below stay inside these ranges and needn't reach their ends.
All inputs are finite; a program needn't handle non-finite values.
Results may differ from the reference program's by a relative error of at most 0.00002.
Values sent between devices are 32-bit elements; how exact they have to be, the bound alone decides.
A program may use at most 64 MiB of HBM per device.

```python
import jax
import jax.numpy as jnp

NT = 512
NI = 256
NX = 512


def rising_field(key, salt):
    keys = jax.random.split(jax.random.fold_in(key, salt), 1)
    inline = jnp.arange(NI, dtype=jnp.float32)[:, None, None]
    ramp = jnp.sqrt(3.0) ** (inline / max(NI - 1, 1))
    base = jnp.clip(jax.random.normal(keys[0], (NI, NX, NT), jnp.float32), -6.0, 6.0)
    return (ramp * base).astype(jnp.float32)


def draw_residual(key, part):
    return rising_field(key, 11)


def draw_direction(key, part):
    return rising_field(key, 23)


def levels(rng, extent, shards, smallest, largest):
    loudness, own = 1.0, jax.random.fold_in(rng, 6)
    for axis_at, parts in shards:
        heights = jnp.exp(jax.random.uniform(jax.random.fold_in(own, axis_at), (parts,), jnp.float32, smallest / len(shards), largest / len(shards)))
        loudness = loudness * jnp.repeat(heights, extent[axis_at] // parts).reshape([-1 if axis == axis_at else 1 for axis in range(len(extent))])
    return loudness


def bell_draw(own_key, shape, deviation, most, shards=(), kind=jnp.bfloat16):
    values = jax.random.normal(own_key, shape, jnp.float32) * deviation
    if len(shards) > 0:
        values = levels(own_key, shape, shards, -0.22, 0.18) * values
    return jnp.clip(values, min=-most, max=most).astype(kind)


def setup_inputs(seed: int = 0) -> dict:
    key_list = jax.random.split(jax.random.key(seed), 7)
    solution = bell_draw(key_list[0], (NI, NX, NT), 1.0, 6.0, ((0, 64), (1, 8)), jnp.float32)
    residual = draw_residual(jax.random.fold_in(key_list[6], 71), 0)
    direction = draw_direction(jax.random.fold_in(key_list[6], 71), 0)
    slope_il = jnp.clip(jax.random.uniform(key_list[3], (NI, NX, NT), jnp.float32, -1.5, 1.5) * levels(key_list[3], (NI, NX, NT), ((0, 64), (1, 8)), -0.4, 0.0), -1.5, 1.5)
    slope_xl = jnp.clip(jax.random.uniform(key_list[4], (NI, NX, NT), jnp.float32, -1.5, 1.5) * levels(key_list[4], (NI, NX, NT), ((0, 64), (1, 8)), -0.4, 0.0), -1.5, 1.5)
    weights = jnp.clip(0.2 + 0.8 * jax.random.uniform(key_list[5], (NI, NX, NT), jnp.float32) ** levels(key_list[5], (NI, NX, NT), ((0, 64), (1, 8)), -0.2, 0.2), 0.2, 1.0)
    return {"solution": solution, "residual": residual, "direction": direction, "slope_il": slope_il, "slope_xl": slope_xl, "weights": weights}


damping = 0.3


def time_diff(field):
    padded = jnp.pad(field, ((0, 0), (0, 0), (1, 1)))
    return 0.5 * (padded[:, :, 2:] - padded[:, :, :-2])


def normal_apply(direction, slope_il, slope_xl, weights):
    squared = weights * weights
    keep_il = jnp.arange(direction.shape[0])[:, None, None] < direction.shape[0] - 1
    keep_xl = jnp.arange(direction.shape[1])[None, :, None] < direction.shape[1] - 1
    ahead_il = jnp.concatenate([direction[1:], jnp.zeros_like(direction[:1])], 0)
    ahead_xl = jnp.concatenate([direction[:, 1:], jnp.zeros_like(direction[:, :1])], 1)
    slope_t = time_diff(direction)
    flux_il = jnp.where(keep_il, squared * (ahead_il - direction - slope_il * slope_t), 0.0)
    flux_xl = jnp.where(keep_xl, squared * (ahead_xl - direction - slope_xl * slope_t), 0.0)
    behind_il = jnp.concatenate([jnp.zeros_like(flux_il[:1]), flux_il[:-1]], 0)
    behind_xl = jnp.concatenate([jnp.zeros_like(flux_xl[:, :1]), flux_xl[:, :-1]], 1)
    term_il = behind_il - flux_il + time_diff(slope_il * flux_il)
    term_xl = behind_xl - flux_xl + time_diff(slope_xl * flux_xl)
    return term_il + term_xl + damping * direction


def reference(solution, residual, direction, slope_il, slope_xl, weights):
    image = normal_apply(direction, slope_il, slope_xl, weights)
    norm_old = jnp.sum(residual * residual)
    alpha = norm_old / jnp.sum(direction * image)
    new_solution = solution + alpha * direction
    new_residual = residual - alpha * image
    norm_new = jnp.sum(new_residual * new_residual)
    new_direction = new_residual + (norm_new / norm_old) * direction
    return new_solution, new_residual, new_direction
```

```python
import jax
import jax.numpy as jnp
from jax import lax
from jax.experimental import pallas as pl
from jax.experimental.pallas import tpu as pltpu
from jax.sharding import PartitionSpec as P

damping = 0.3
F32 = jnp.float32
MESH_ID = pl.DeviceIdType.MESH

NIL, NXL = 64, 8
ROWS, COLS, NT = 4, 64, 512
STRIPS = COLS // 8
CHUNKS = 4
CHUNK = COLS // CHUNKS


def kernel(
    res_hbm, u_hbm, sil_hbm, sxl_hbm, w_hbm,
    image, coef,
    res, u, sil, sxl, w, fil, fx, h, xl_u_out, xl_u_in, xl_f_out, xl_f_in,
    msg, box,
    load_sem, us_send, us_recv, fs_send, fs_recv, x_send, x_recv, r_send, r_recv,
):
    il, xl = lax.axis_index("il"), lax.axis_index("xl")
    z_hi, y, core = il // 16, (il // 2) % 8, il % 2
    z_lo, x = xl // 4, xl % 4
    next_il = ((il + 1) % NIL, xl)
    prev_il = ((il + NIL - 1) % NIL, xl)
    next_xl = (il, (xl + 1) % NXL)
    prev_xl = (il, (xl + NXL - 1) % NXL)
    near = x * 2 + core
    z = z_hi * 2 + z_lo

    def peer(phase, d):
        if phase == 0:
            k = (near + d) % 8
            return (il - core + k % 2, z_lo * 4 + k // 2)
        if phase == 1:
            return (z_hi * 16 + ((y + d) % 8) * 2 + core, xl)
        k = (z + d) % 8
        return ((k // 2) * 16 + y * 2 + core, (k % 2) * 4 + x)

    order = (4, 3, 5, 2, 6, 1, 7)
    barrier = pltpu.get_barrier_semaphore()
    peers = [next_il, prev_il, next_xl, prev_xl]
    peers += [peer(phase, d) for phase in (2, 1, 0) for d in order]
    for other in peers:
        pl.semaphore_signal(barrier, inc=1, device_id=other, device_id_type=MESH_ID)

    loads = [
        pltpu.make_async_copy(u_hbm, u.at[pl.ds(0, ROWS), pl.ds(0, COLS)], load_sem.at[0]),
        pltpu.make_async_copy(w_hbm, w, load_sem.at[1]),
        pltpu.make_async_copy(sxl_hbm, sxl, load_sem.at[2]),
        pltpu.make_async_copy(sil_hbm, sil, load_sem.at[3]),
        pltpu.make_async_copy(res_hbm, res, load_sem.at[4]),
    ]
    for load in loads:
        load.start()
    pl.semaphore_wait(barrier, len(peers))

    u_copies = []
    for c in range(CHUNKS):
        u_copies.append(pltpu.make_async_remote_copy(
            u_hbm.at[0, pl.ds(c * CHUNK, CHUNK)],
            u.at[ROWS, pl.ds(c * CHUNK, CHUNK)],
            us_send.at[c], us_recv.at[c], prev_il, MESH_ID,
        ))
        u_copies[c].start()

    lane = lax.broadcasted_iota(jnp.int32, (8, NT), 1)
    sub = lax.broadcasted_iota(jnp.int32, (8, NT), 0)
    first_t, last_t = lane == 0, lane == NT - 1
    first_r, last_r = sub == 0, sub == 7

    def diff_t(v):
        ahead = jnp.where(last_t, 0.0, pltpu.roll(v, NT - 1, 1))
        behind = jnp.where(first_t, 0.0, pltpu.roll(v, 1, 1))
        return 0.5 * (ahead - behind)

    loads[0].wait()
    for i in range(ROWS):
        xl_u_out[i:i + 1] = u[i, 0:1]
    x_u = pltpu.make_async_remote_copy(
        xl_u_out, xl_u_in, x_send.at[0], x_recv.at[0], prev_xl, MESH_ID)
    x_u.start()
    loads[1].wait()
    loads[2].wait()
    for i in range(ROWS):
        tail = slice(COLS - 8, COLS)
        g = u[i, tail] + sxl[i, tail] * diff_t(u[i, tail])
        wt = w[i, tail]
        xl_f_out[i:i + 1] = g[7:8]
        xl_f_out[ROWS + i:ROWS + i + 1] = (wt * wt)[7:8]
    x_f = pltpu.make_async_remote_copy(
        xl_f_out, xl_f_in, x_send.at[1], x_recv.at[1], next_xl, MESH_ID)
    x_f.start()
    loads[3].wait()

    keep_il = jnp.where(il == NIL - 1, 0.0, 1.0).astype(F32)
    keep_xl = jnp.where(xl == NXL - 1, 0.0, 1.0).astype(F32)
    had_il = jnp.where(il == 0, 0.0, 1.0).astype(F32)
    had_xl = jnp.where(xl == 0, 0.0, 1.0).astype(F32)

    def crossline_flux(i, rows, next_row, last=False):
        here = u[i, rows]
        t = diff_t(here)
        wt = w[i, rows]
        sq = wt * wt
        ahead = jnp.where(last_r, next_row, pltpu.roll(here, 7, 0))
        slope = sxl[i, rows]
        flux = sq * (ahead - here - slope * t)
        if last:
            flux = jnp.where(last_r, keep_xl * flux, flux)
        return here, t, sq, flux, slope * flux

    def put_strip(i, jb, next_row, last=False):
        start = jb * 8 if last else pl.multiple_of(jb * 8, 8)
        rows = pl.ds(start, 8)
        here, t, sq, flux, part = crossline_flux(i, rows, next_row, last)
        fx[i, pl.ds(start + 8, 8)] = flux
        slope = sil[i, rows]
        if i < ROWS - 1:
            f = sq * (u[i + 1, rows] - here - slope * t)
            fil[i + 1, rows] = f
            h[i, rows] = part + slope * f
        else:
            fil[i + 1, rows] = here + slope * t
            h[i, rows] = part

    for i in range(ROWS):
        def strip(jb, _, i=i):
            put_strip(i, jb, u[i, pl.ds(jb * 8 + 8, 1)])
            return 0
        lax.fori_loop(0, STRIPS - 1, strip, 0, unroll=True)

    x_u.wait_recv()
    x_f.wait_recv()
    for i in range(ROWS):
        put_strip(i, STRIPS - 1, xl_u_in[i:i + 1], True)
        fx[i, 7:8] = had_xl * (xl_f_in[ROWS + i:ROWS + i + 1] * (u[i, 0:1] - xl_f_in[i:i + 1]))

    f_copies = []
    for c in range(CHUNKS):
        u_copies[c].wait_recv()
        for s in range(CHUNK // 8):
            rows = pl.ds(c * CHUNK + s * 8, 8)
            wt = w[ROWS - 1, rows]
            f = keep_il * (wt * wt * (u[ROWS, rows] - fil[ROWS, rows]))
            fil[ROWS, rows] = f
            h[ROWS - 1, rows] = h[ROWS - 1, rows] + sil[ROWS - 1, rows] * f
        f_copies.append(pltpu.make_async_remote_copy(
            fil.at[ROWS, pl.ds(c * CHUNK, CHUNK)],
            fil.at[0, pl.ds(c * CHUNK, CHUNK)],
            fs_send.at[c], fs_recv.at[c], next_il, MESH_ID,
        ))
        f_copies[c].start()
    loads[4].wait()

    def image_strip(i, jb, sums, scale=None):
        rows = pl.ds(pl.multiple_of(jb * 8, 8), 8)
        fx_here = fx[i, pl.ds(pl.multiple_of(jb * 8 + 8, 8), 8)]
        fx_behind = jnp.where(first_r, fx[i, pl.ds(jb * 8 + 7, 1)], pltpu.roll(fx_here, 1, 0))
        before = fil[i, rows]
        if scale is not None:
            before = scale * before
        here = u[i, rows]
        q = (before - fil[i + 1, rows]) + (fx_behind - fx_here) + diff_t(h[i, rows]) + damping * here
        image[i, rows] = q
        r = res[i, rows]
        rr, dq, rq, qq = sums
        return rr + r * r, dq + here * q, rq + r * q, qq + q * q

    sums = tuple(jnp.zeros((8, NT), F32) for _ in range(4))
    for i in range(1, ROWS):
        sums = lax.fori_loop(0, STRIPS, lambda jb, s, i=i: image_strip(i, jb, s), sums, unroll=True)
    for c in range(CHUNKS):
        f_copies[c].wait_recv()
        sums = lax.fori_loop(
            c * CHUNK // 8, (c + 1) * CHUNK // 8,
            lambda jb, s: image_strip(0, jb, s, had_il), sums, unroll=True)

    lane1 = lax.broadcasted_iota(jnp.int32, (8, 128), 1)
    row = jnp.zeros((8, 128), F32)
    for k, total in enumerate(sums):
        v = total[:, 0:128] + total[:, 128:256] + total[:, 256:384] + total[:, 384:512]
        v = v + pltpu.roll(v, 64, 1)
        v = v + pltpu.roll(v, 32, 1)
        row = jnp.where(lane1 // 32 == k, v, row)
    row = jnp.sum(row, axis=0, keepdims=True)

    for phase in range(3):
        msg[phase, 0:1] = row
        box[phase, 7:8] = row
        for d in order:
            pltpu.make_async_remote_copy(
                msg.at[phase, pl.ds(0, 1)], box.at[phase, pl.ds(d - 1, 1)],
                r_send.at[phase], r_recv.at[phase], peer(phase, d), MESH_ID,
            ).start()
        drain = pltpu.make_async_remote_copy(
            box.at[phase, pl.ds(0, 7)], box.at[phase, pl.ds(0, 7)],
            r_send.at[phase], r_recv.at[phase], peer(phase, 1), MESH_ID)
        drain.wait_recv()
        row = jnp.sum(box[phase], axis=0, keepdims=True)

    full = jnp.broadcast_to(row, (8, 128))
    rr, dq, rq, qq = (
        jnp.sum(jnp.where(lane1 // 32 == k, full, 0.0), axis=1, keepdims=True) for k in range(4))
    alpha = rr / dq
    beta = (rr - 2.0 * alpha * rq + alpha * alpha * qq) / rr
    coef[...] = jnp.where(lane1 == 0, alpha, beta)

    for copy in u_copies + f_copies:
        copy.wait_send()
    x_u.wait_send()
    x_f.wait_send()
    for phase in range(3):
        pltpu.make_async_remote_copy(
            box.at[phase, pl.ds(0, 7)], box.at[phase, pl.ds(0, 7)],
            r_send.at[phase], r_recv.at[phase], peer(phase, 1), MESH_ID).wait_send()


def apply(residual, direction, slope_il, slope_xl, weights):
    hbm, vmem = pl.BlockSpec(memory_space=pltpu.HBM), pl.BlockSpec(memory_space=pltpu.VMEM)
    block = (ROWS, COLS, NT)
    dma = pltpu.SemaphoreType.DMA
    return pl.pallas_call(
        kernel,
        out_shape=(jax.ShapeDtypeStruct(block, F32), jax.ShapeDtypeStruct((8, 128), F32)),
        in_specs=[hbm] * 5,
        out_specs=(vmem, vmem),
        scratch_shapes=[
            pltpu.VMEM(block, F32),
            pltpu.VMEM((ROWS + 1, COLS + 8, NT), F32),
            pltpu.VMEM(block, F32),
            pltpu.VMEM(block, F32),
            pltpu.VMEM(block, F32),
            pltpu.VMEM((ROWS + 1, COLS, NT), F32),
            pltpu.VMEM((ROWS, COLS + 8, NT), F32),
            pltpu.VMEM(block, F32),
            pltpu.VMEM((ROWS, NT), F32),
            pltpu.VMEM((ROWS, NT), F32),
            pltpu.VMEM((2 * ROWS, NT), F32),
            pltpu.VMEM((2 * ROWS, NT), F32),
            pltpu.VMEM((3, 8, 128), F32),
            pltpu.VMEM((3, 8, 128), F32),
            dma((5,)),
            dma((CHUNKS,)), dma((CHUNKS,)), dma((CHUNKS,)), dma((CHUNKS,)),
            dma((2,)), dma((2,)), dma((3,)), dma((3,)),
        ],
        compiler_params=pltpu.CompilerParams(
            collective_id=0, has_side_effects=True, vmem_limit_bytes=24 * 2**20),
    )(residual, direction, slope_il, slope_xl, weights)


def body(solution, residual, direction, slope_il, slope_xl, weights):
    image, coef = apply(residual, direction, slope_il, slope_xl, weights)
    alpha, beta = coef[0, 0], coef[0, 1]
    new_solution = solution + alpha * direction
    new_residual = residual - alpha * image
    new_direction = new_residual + beta * direction
    return new_solution, new_residual, new_direction


def solution(mesh):
    spec = P("il", "xl", None)
    return jax.shard_map(
        body, mesh=mesh, in_specs=(spec,) * 6, out_specs=(spec,) * 3, check_vma=False)
```

```python
import jax
import jax.numpy as jnp
from jax import lax
from jax.experimental import pallas as pl
from jax.experimental.pallas import tpu as pltpu
from jax.sharding import PartitionSpec as P

damping = 0.3
F32 = jnp.float32
MESH_ID = pl.DeviceIdType.MESH

NIL, NXL = 64, 8
ROWS, COLS, NT = 4, 64, 512
STRIPS = COLS // 8


def kernel(
    sol_hbm, res_hbm, u_hbm, sil_hbm, sxl_hbm, w_hbm,
    sol, res, u, image, coef,
    sil, sxl, w, fil, fx, h, u_in, w_in, g_out, g_in, xl_u_out, xl_u_in, xl_f_out, xl_f_in,
    msg, box,
    load_sem, i_send, i_recv, x_send, x_recv, r_send, r_recv,
):
    il, xl = lax.axis_index("il"), lax.axis_index("xl")
    z_hi, y, core = il // 16, (il // 2) % 8, il % 2
    z_lo, x = xl // 4, xl % 4
    next_il = ((il + 1) % NIL, xl)
    prev_il = ((il + NIL - 1) % NIL, xl)
    next_xl = (il, (xl + 1) % NXL)
    prev_xl = (il, (xl + NXL - 1) % NXL)
    near = x * 2 + core
    z = z_hi * 2 + z_lo

    def peer(phase, d):
        if phase == 0:
            k = (near + d) % 8
            return (il - core + k % 2, z_lo * 4 + k // 2)
        if phase == 1:
            return (z_hi * 16 + ((y + d) % 8) * 2 + core, xl)
        k = (z + d) % 8
        return ((k // 2) * 16 + y * 2 + core, (k % 2) * 4 + x)

    order = (4, 3, 5, 2, 6, 1, 7)
    barrier = pltpu.get_barrier_semaphore()
    peers = [next_il, prev_il, next_xl, prev_xl]
    peers += [peer(phase, d) for phase in (2, 1, 0) for d in order]
    for other in peers:
        pl.semaphore_signal(barrier, inc=1, device_id=other, device_id_type=MESH_ID)

    loads = [
        pltpu.make_async_copy(source, target, load_sem.at[k])
        for k, (source, target) in enumerate((
            (u_hbm, u), (sil_hbm, sil), (w_hbm, w), (sxl_hbm, sxl), (res_hbm, res), (sol_hbm, sol)))
    ]
    for load in loads:
        load.start()
    pl.semaphore_wait(barrier, len(peers))

    i_u = pltpu.make_async_remote_copy(
        u_hbm.at[0], u_in, i_send.at[0], i_recv.at[0], prev_il, MESH_ID)
    i_u.start()
    i_w = pltpu.make_async_remote_copy(
        w_hbm.at[ROWS - 1], w_in, i_send.at[1], i_recv.at[1], next_il, MESH_ID)
    i_w.start()

    lane = lax.broadcasted_iota(jnp.int32, (8, NT), 1)
    sub = lax.broadcasted_iota(jnp.int32, (8, NT), 0)
    first_t, last_t = lane == 0, lane == NT - 1
    first_r, last_r = sub == 0, sub == 7

    def diff_t(v):
        ahead = jnp.where(last_t, 0.0, pltpu.roll(v, NT - 1, 1))
        behind = jnp.where(first_t, 0.0, pltpu.roll(v, 1, 1))
        return 0.5 * (ahead - behind)

    loads[0].wait()
    loads[1].wait()

    def lean(jb, _):
        rows = pl.ds(pl.multiple_of(jb * 8, 8), 8)
        here = u[ROWS - 1, rows]
        g_out[rows] = here + sil[ROWS - 1, rows] * diff_t(here)
        return 0
    lax.fori_loop(0, STRIPS, lean, 0, unroll=True)
    i_g = pltpu.make_async_remote_copy(g_out, g_in, i_send.at[2], i_recv.at[2], next_il, MESH_ID)
    i_g.start()

    for i in range(ROWS):
        xl_u_out[i:i + 1] = u[i, 0:1]
    x_u = pltpu.make_async_remote_copy(
        xl_u_out, xl_u_in, x_send.at[0], x_recv.at[0], prev_xl, MESH_ID)
    x_u.start()
    loads[2].wait()
    loads[3].wait()
    for i in range(ROWS):
        tail = slice(COLS - 8, COLS)
        g = u[i, tail] + sxl[i, tail] * diff_t(u[i, tail])
        xl_f_out[i:i + 1] = g[7:8]
        xl_f_out[ROWS + i:ROWS + i + 1] = w[i, tail][7:8]
    x_f = pltpu.make_async_remote_copy(
        xl_f_out, xl_f_in, x_send.at[1], x_recv.at[1], next_xl, MESH_ID)
    x_f.start()

    keep_il = jnp.where(il == NIL - 1, 0.0, 1.0).astype(F32)
    keep_xl = jnp.where(xl == NXL - 1, 0.0, 1.0).astype(F32)
    had_il = jnp.where(il == 0, 0.0, 1.0).astype(F32)
    had_xl = jnp.where(xl == 0, 0.0, 1.0).astype(F32)

    def put_strip(i, jb, next_row, last=False):
        start = pl.multiple_of(jb * 8, 8)
        rows = pl.ds(start, 8)
        here = u[i, rows]
        t = diff_t(here)
        wt = w[i, rows]
        sq = wt * wt
        ahead = jnp.where(last_r, next_row, pltpu.roll(here, 7, 0))
        slope = sxl[i, rows]
        flux = sq * (ahead - here - slope * t)
        if last:
            flux = jnp.where(last_r, keep_xl * flux, flux)
        fx[i, pl.ds(start + 8, 8)] = flux
        part = slope * flux
        if i < ROWS - 1:
            slope = sil[i, rows]
            f = sq * (u[i + 1, rows] - here - slope * t)
            fil[i, rows] = f
            part = part + slope * f
        h[i, rows] = part

    for i in range(ROWS):
        def strip(jb, _, i=i):
            put_strip(i, jb, u[i, pl.ds(jb * 8 + 8, 1)])
            return 0
        lax.fori_loop(0, STRIPS - 1, strip, 0, unroll=True)

    x_u.wait_recv()
    for i in range(ROWS):
        put_strip(i, STRIPS - 1, xl_u_in[i:i + 1], True)
    x_f.wait_recv()
    for i in range(ROWS):
        wt = xl_f_in[ROWS + i:ROWS + i + 1]
        fx[i, 7:8] = had_xl * (wt * wt * (u[i, 0:1] - xl_f_in[i:i + 1]))
    loads[4].wait()

    def image_strip(i, jb, sums):
        rows = pl.ds(pl.multiple_of(jb * 8, 8), 8)
        fx_here = fx[i, pl.ds(pl.multiple_of(jb * 8 + 8, 8), 8)]
        fx_behind = jnp.where(first_r, fx[i, pl.ds(jb * 8 + 7, 1)], pltpu.roll(fx_here, 1, 0))
        here = u[i, rows]
        if i == 0:
            wt = w_in[rows]
            before = had_il * (wt * wt * (here - g_in[rows]))
        else:
            before = fil[i - 1, rows]
        q = (before - fil[i, rows]) + (fx_behind - fx_here) + diff_t(h[i, rows]) + damping * here
        image[i, rows] = q
        r = res[i, rows]
        rr, dq, rq, qq = sums
        return rr + r * r, dq + here * q, rq + r * q, qq + q * q

    def image_inline(i, sums):
        return lax.fori_loop(0, STRIPS, lambda jb, s: image_strip(i, jb, s), sums, unroll=True)

    sums = tuple(jnp.zeros((8, NT), F32) for _ in range(4))
    for i in range(1, ROWS - 1):
        sums = image_inline(i, sums)

    i_u.wait_recv()

    def last_inline(jb, _):
        rows = pl.ds(pl.multiple_of(jb * 8, 8), 8)
        wt = w[ROWS - 1, rows]
        f = keep_il * (wt * wt * (u_in[rows] - g_out[rows]))
        fil[ROWS - 1, rows] = f
        h[ROWS - 1, rows] = h[ROWS - 1, rows] + sil[ROWS - 1, rows] * f
        return 0
    lax.fori_loop(0, STRIPS, last_inline, 0, unroll=True)
    sums = image_inline(ROWS - 1, sums)

    i_w.wait_recv()
    i_g.wait_recv()
    sums = image_inline(0, sums)

    lane1 = lax.broadcasted_iota(jnp.int32, (8, 128), 1)
    row = jnp.zeros((8, 128), F32)
    for k, total in enumerate(sums):
        v = total[:, 0:128] + total[:, 128:256] + total[:, 256:384] + total[:, 384:512]
        v = v + pltpu.roll(v, 64, 1)
        v = v + pltpu.roll(v, 32, 1)
        row = jnp.where(lane1 // 32 == k, v, row)
    row = jnp.sum(row, axis=0, keepdims=True)

    for phase in range(3):
        msg[phase, 0:1] = row
        box[phase, 7:8] = row
        for d in order:
            pltpu.make_async_remote_copy(
                msg.at[phase, pl.ds(0, 1)], box.at[phase, pl.ds(d - 1, 1)],
                r_send.at[phase], r_recv.at[phase], peer(phase, d), MESH_ID,
            ).start()
        drain = pltpu.make_async_remote_copy(
            box.at[phase, pl.ds(0, 7)], box.at[phase, pl.ds(0, 7)],
            r_send.at[phase], r_recv.at[phase], peer(phase, 1), MESH_ID)
        drain.wait_recv()
        row = jnp.sum(box[phase], axis=0, keepdims=True)

    full = jnp.broadcast_to(row, (8, 128))
    rr, dq, rq, qq = (
        jnp.sum(jnp.where(lane1 // 32 == k, full, 0.0), axis=1, keepdims=True) for k in range(4))
    alpha = rr / dq
    beta = (rr - 2.0 * alpha * rq + alpha * alpha * qq) / rr
    coef[...] = jnp.where(lax.broadcasted_iota(jnp.int32, (8, 128), 0) == 0, alpha, beta)

    for copy in (i_u, i_w, i_g, x_u, x_f):
        copy.wait_send()
    for phase in range(3):
        pltpu.make_async_remote_copy(
            box.at[phase, pl.ds(0, 7)], box.at[phase, pl.ds(0, 7)],
            r_send.at[phase], r_recv.at[phase], peer(phase, 1), MESH_ID).wait_send()
    loads[5].wait()


def apply(solution, residual, direction, slope_il, slope_xl, weights):
    hbm, vmem = pl.BlockSpec(memory_space=pltpu.HBM), pl.BlockSpec(memory_space=pltpu.VMEM)
    block, plane, line = (ROWS, COLS, NT), (COLS, NT), (ROWS, NT)
    dma = pltpu.SemaphoreType.DMA
    operands = (
        pltpu.with_memory_space_constraint(v, pltpu.HBM)
        for v in (solution, residual, direction, slope_il, slope_xl, weights))
    return pl.pallas_call(
        kernel,
        out_shape=(jax.ShapeDtypeStruct(block, F32),) * 4 + (jax.ShapeDtypeStruct((8, 128), F32),),
        in_specs=[hbm] * 6,
        out_specs=(vmem,) * 5,
        scratch_shapes=[
            pltpu.VMEM(shape, F32)
            for shape in (
                block, block, block, block, (ROWS, COLS + 8, NT), block, plane, plane, plane, plane,
                line, line, (2 * ROWS, NT), (2 * ROWS, NT), (3, 8, 128), (3, 8, 128))
        ] + [dma((6,)), dma((3,)), dma((3,)), dma((2,)), dma((2,)), dma((3,)), dma((3,))],
        compiler_params=pltpu.CompilerParams(
            collective_id=0, has_side_effects=True, vmem_limit_bytes=24 * 2**20),
    )(*operands)


def update_kernel(sol, res, u, image, coef, new_sol_hbm, new_res_hbm, new_dir_hbm, outs, sems):
    alpha = jnp.broadcast_to(coef[0:1, 0:128], (8, 128))
    beta = jnp.broadcast_to(coef[1:2, 0:128], (8, 128))
    alpha = jnp.concatenate([alpha] * (NT // 128), axis=1)
    beta = jnp.concatenate([beta] * (NT // 128), axis=1)
    copies = []
    for i in range(ROWS):
        def strip(jb, _, i=i):
            rows = pl.ds(pl.multiple_of(jb * 8, 8), 8)
            here = u[i, rows]
            r = res[i, rows] - alpha * image[i, rows]
            outs[0, i, rows] = sol[i, rows] + alpha * here
            outs[1, i, rows] = r
            outs[2, i, rows] = r + beta * here
            return 0
        lax.fori_loop(0, STRIPS, strip, 0, unroll=True)
        for k, target in enumerate((new_sol_hbm, new_res_hbm, new_dir_hbm)):
            copies.append(pltpu.make_async_copy(outs.at[k, i], target.at[i], sems.at[k, i]))
            copies[-1].start()
    for copy in copies:
        copy.wait()


def update(sol, res, u, image, coef):
    hbm, vmem = pl.BlockSpec(memory_space=pl.ANY), pl.BlockSpec(memory_space=pltpu.VMEM)
    block = (ROWS, COLS, NT)
    return pl.pallas_call(
        update_kernel,
        out_shape=(jax.ShapeDtypeStruct(block, F32),) * 3,
        in_specs=[vmem] * 5,
        out_specs=(hbm,) * 3,
        scratch_shapes=[pltpu.VMEM((3,) + block, F32), pltpu.SemaphoreType.DMA((3, ROWS))],
        compiler_params=pltpu.CompilerParams(vmem_limit_bytes=8 * 2**20),
    )(sol, res, u, image, coef)


def body(solution, residual, direction, slope_il, slope_xl, weights):
    return update(*apply(solution, residual, direction, slope_il, slope_xl, weights))


def solution(mesh):
    spec = P("il", "xl", None)
    return jax.shard_map(
        body, mesh=mesh, in_specs=(spec,) * 6, out_specs=(spec,) * 3, check_vma=False)
```

```python
import jax
import jax.numpy as jnp
from jax import lax
from jax.experimental import pallas as pl
from jax.experimental.pallas import tpu as pltpu
from jax.sharding import PartitionSpec as P

damping = 0.3
F32 = jnp.float32
MESH_ID = pl.DeviceIdType.MESH

NIL, NXL = 64, 8
ROWS, COLS, NT = 4, 64, 512
STRIPS = COLS // 8


def kernel(
    sol_hbm, res_hbm, u_hbm, sil_hbm, sxl_hbm, w_hbm,
    sol, res, u, image, coef,
    sil, sxl, w, fil, fx, h, u_in, w_in, g_out, g_in, xl_u_out, xl_u_in, xl_f_out, xl_f_in,
    msg, box_xy, box_zc,
    load_sem, i_send, i_recv, x_send, x_recv, r_send, r_recv, go,
):
    il, xl = lax.axis_index("il"), lax.axis_index("xl")
    z_hi, y, core = il // 16, (il // 2) % 8, il % 2
    z_lo, x = xl // 4, xl % 4
    z = z_hi * 2 + z_lo

    def at(dx=0, dy=0, dz=0, dc=0):
        nz = (z + dz) % 8
        return ((nz // 2) * 16 + ((y + dy) % 8) * 2 + (core + dc) % 2, (nz % 2) * 4 + (x + dx) % 4)

    def along(il_by, xl_by=0):
        return ((il + il_by + NIL) % NIL, (xl + xl_by + NXL) % NXL)

    next_il, prev_il, next_xl, prev_xl = along(1), along(-1), along(0, 1), along(0, -1)
    sibling = at(dc=1)

    barrier = pltpu.get_barrier_semaphore()
    neighbours = [at(dx=1), at(dx=3), at(dy=1), at(dy=7), at(dz=1), at(dz=7)]
    peers = [next_il, prev_il, along(2), along(-2), next_xl, prev_xl] + neighbours
    steps = (
        neighbours,
        [at(dy=2), at(dy=6), at(dz=2), at(dz=6)],
        [at(dx=1), at(dx=2), at(dx=3), sibling],
    )
    for other in peers:
        pl.semaphore_signal(barrier, inc=1, device_id=other, device_id_type=MESH_ID)

    def say(step):
        for other in steps[step]:
            pl.semaphore_signal(go.at[step], inc=1, device_id=other, device_id_type=MESH_ID)

    def hear(step):
        pl.semaphore_wait(go.at[step], len(steps[step]))

    loads = [
        pltpu.make_async_copy(source, target, load_sem.at[k])
        for k, (source, target) in enumerate((
            (u_hbm, u), (sil_hbm, sil), (w_hbm, w), (sxl_hbm, sxl), (res_hbm, res), (sol_hbm, sol)))
    ]
    for load in loads:
        load.start()
    pl.semaphore_wait(barrier, len(peers))

    i_u = pltpu.make_async_remote_copy(
        u_hbm.at[0], u_in, i_send.at[0], i_recv.at[0], prev_il, MESH_ID)
    i_u.start()
    i_w = pltpu.make_async_remote_copy(
        w_hbm.at[ROWS - 1], w_in.at[1], i_send.at[1], i_recv.at[1], sibling, MESH_ID)
    i_w.start()
    relay = pltpu.make_async_remote_copy(
        w_in.at[1], w_in.at[0], i_send.at[3], i_recv.at[3], along(2), MESH_ID)
    say(0)

    lane = lax.broadcasted_iota(jnp.int32, (8, NT), 1)
    sub = lax.broadcasted_iota(jnp.int32, (8, NT), 0)
    first_t, last_t = lane == 0, lane == NT - 1
    first_r, last_r = sub == 0, sub == 7

    def diff_t(v):
        ahead = jnp.where(last_t, 0.0, pltpu.roll(v, NT - 1, 1))
        behind = jnp.where(first_t, 0.0, pltpu.roll(v, 1, 1))
        return 0.5 * (ahead - behind)

    loads[0].wait()
    loads[1].wait()

    def lean(jb, _):
        rows = pl.ds(pl.multiple_of(jb * 8, 8), 8)
        here = u[ROWS - 1, rows]
        g_out[rows] = here + sil[ROWS - 1, rows] * diff_t(here)
        return 0
    lax.fori_loop(0, STRIPS, lean, 0, unroll=True)
    i_g = pltpu.make_async_remote_copy(g_out, g_in, i_send.at[2], i_recv.at[2], next_il, MESH_ID)
    i_g.start()

    @pl.when(core == 0)
    def _():
        i_w.wait_recv()
        relay.start()


    for i in range(ROWS):
        xl_u_out[i:i + 1] = u[i, 0:1]
    x_u = pltpu.make_async_remote_copy(
        xl_u_out, xl_u_in, x_send.at[0], x_recv.at[0], prev_xl, MESH_ID)
    x_u.start()
    loads[2].wait()
    loads[3].wait()
    for i in range(ROWS):
        tail = slice(COLS - 8, COLS)
        g = u[i, tail] + sxl[i, tail] * diff_t(u[i, tail])
        xl_f_out[i:i + 1] = g[7:8]
        xl_f_out[ROWS + i:ROWS + i + 1] = w[i, tail][7:8]
    x_f = pltpu.make_async_remote_copy(
        xl_f_out, xl_f_in, x_send.at[1], x_recv.at[1], next_xl, MESH_ID)
    x_f.start()
    hear(0)
    say(1)

    keep_il = jnp.where(il == NIL - 1, 0.0, 1.0).astype(F32)
    keep_xl = jnp.where(xl == NXL - 1, 0.0, 1.0).astype(F32)
    had_il = jnp.where(il == 0, 0.0, 1.0).astype(F32)
    had_xl = jnp.where(xl == 0, 0.0, 1.0).astype(F32)

    def put_strip(i, jb, next_row, last=False):
        start = pl.multiple_of(jb * 8, 8)
        rows = pl.ds(start, 8)
        here = u[i, rows]
        t = diff_t(here)
        wt = w[i, rows]
        sq = wt * wt
        ahead = jnp.where(last_r, next_row, pltpu.roll(here, 7, 0))
        slope = sxl[i, rows]
        flux = sq * (ahead - here - slope * t)
        if last:
            flux = jnp.where(last_r, keep_xl * flux, flux)
        fx[i, pl.ds(start + 8, 8)] = flux
        part = slope * flux
        if i < ROWS - 1:
            slope = sil[i, rows]
            f = sq * (u[i + 1, rows] - here - slope * t)
            fil[i, rows] = f
            part = part + slope * f
        h[i, rows] = part

    for i in range(ROWS):
        def strip(jb, _, i=i):
            put_strip(i, jb, u[i, pl.ds(jb * 8 + 8, 1)])
            return 0
        lax.fori_loop(0, STRIPS - 1, strip, 0, unroll=True)

    hear(1)
    say(2)

    x_u.wait_recv()
    for i in range(ROWS):
        put_strip(i, STRIPS - 1, xl_u_in[i:i + 1], True)
    x_f.wait_recv()
    for i in range(ROWS):
        wt = xl_f_in[ROWS + i:ROWS + i + 1]
        fx[i, 7:8] = had_xl * (wt * wt * (u[i, 0:1] - xl_f_in[i:i + 1]))
    loads[4].wait()

    def image_strip(i, jb, sums):
        rows = pl.ds(pl.multiple_of(jb * 8, 8), 8)
        fx_here = fx[i, pl.ds(pl.multiple_of(jb * 8 + 8, 8), 8)]
        fx_behind = jnp.where(first_r, fx[i, pl.ds(jb * 8 + 7, 1)], pltpu.roll(fx_here, 1, 0))
        here = u[i, rows]
        if i == 0:
            wt = w_in[core, rows]
            before = had_il * (wt * wt * (here - g_in[rows]))
        else:
            before = fil[i - 1, rows]
        q = (before - fil[i, rows]) + (fx_behind - fx_here) + diff_t(h[i, rows]) + damping * here
        image[i, rows] = q
        r = res[i, rows]
        rr, dq, rq, qq = sums
        return rr + r * r, dq + here * q, rq + r * q, qq + q * q

    def image_inline(i, sums):
        return lax.fori_loop(0, STRIPS, lambda jb, s: image_strip(i, jb, s), sums, unroll=True)

    sums = tuple(jnp.zeros((8, NT), F32) for _ in range(4))
    for i in range(1, ROWS - 1):
        sums = image_inline(i, sums)

    i_u.wait_recv()

    def last_inline(jb, _):
        rows = pl.ds(pl.multiple_of(jb * 8, 8), 8)
        wt = w[ROWS - 1, rows]
        f = keep_il * (wt * wt * (u_in[rows] - g_out[rows]))
        fil[ROWS - 1, rows] = f
        h[ROWS - 1, rows] = h[ROWS - 1, rows] + sil[ROWS - 1, rows] * f
        return 0
    lax.fori_loop(0, STRIPS, last_inline, 0, unroll=True)
    sums = image_inline(ROWS - 1, sums)

    @pl.when(core == 0)
    def _():
        relay.wait_recv()

    @pl.when(core == 1)
    def _():
        i_w.wait_recv()

    i_g.wait_recv()
    sums = image_inline(0, sums)
    hear(2)

    lane1 = lax.broadcasted_iota(jnp.int32, (8, 128), 1)
    row = jnp.zeros((8, 128), F32)
    for k, total in enumerate(sums):
        v = total[:, 0:128] + total[:, 128:256] + total[:, 256:384] + total[:, 384:512]
        v = v + pltpu.roll(v, 64, 1)
        v = v + pltpu.roll(v, 32, 1)
        row = jnp.where(lane1 // 32 == k, v, row)
    row = jnp.sum(row, axis=0, keepdims=True)

    near = lambda by, size: min(by, size - by)
    plane = [(dx, dy, 0, 0) for dx in range(4) for dy in range(8) if dx + dy > 0]
    plane.sort(key=lambda p: -near(p[0], 4) - near(p[1], 8))
    line = [(0, 0, dz, dc) for dz in range(8) for dc in range(2) if dz + dc > 0]
    line.sort(key=lambda p: -near(p[2], 8))
    drains = []
    for phase, (offsets, box) in enumerate(((plane, box_xy), (line, box_zc))):
        count = len(offsets)
        msg[phase, 0:1] = row
        box[count:count + 1] = row
        for slot, by in enumerate(offsets):
            pltpu.make_async_remote_copy(
                msg.at[phase, pl.ds(0, 1)], box.at[pl.ds(slot, 1)],
                r_send.at[phase], r_recv.at[phase], at(*by), MESH_ID,
            ).start()
        drains.append(pltpu.make_async_remote_copy(
            box.at[pl.ds(0, count)], box.at[pl.ds(0, count)],
            r_send.at[phase], r_recv.at[phase], sibling, MESH_ID))
        drains[phase].wait_recv()
        row = jnp.sum(box[...], axis=0, keepdims=True)

    full = jnp.broadcast_to(row, (8, 128))
    rr, dq, rq, qq = (
        jnp.sum(jnp.where(lane1 // 32 == k, full, 0.0), axis=1, keepdims=True) for k in range(4))
    alpha = rr / dq
    beta = (rr - 2.0 * alpha * rq + alpha * alpha * qq) / rr
    coef[...] = jnp.where(lax.broadcasted_iota(jnp.int32, (8, 128), 0) == 0, alpha, beta)

    for copy in (i_u, i_w, i_g, x_u, x_f):
        copy.wait_send()

    @pl.when(core == 0)
    def _():
        relay.wait_send()

    for drain in drains:
        drain.wait_send()
    loads[5].wait()


def apply(solution, residual, direction, slope_il, slope_xl, weights):
    hbm, vmem = pl.BlockSpec(memory_space=pltpu.HBM), pl.BlockSpec(memory_space=pltpu.VMEM)
    block, plane, line = (ROWS, COLS, NT), (COLS, NT), (ROWS, NT)
    dma = pltpu.SemaphoreType.DMA
    operands = (
        pltpu.with_memory_space_constraint(v, pltpu.HBM)
        for v in (solution, residual, direction, slope_il, slope_xl, weights))
    return pl.pallas_call(
        kernel,
        out_shape=(jax.ShapeDtypeStruct(block, F32),) * 4 + (jax.ShapeDtypeStruct((8, 128), F32),),
        in_specs=[hbm] * 6,
        out_specs=(vmem,) * 5,
        scratch_shapes=[
            pltpu.VMEM(shape, F32)
            for shape in (
                block, block, block, block, (ROWS, COLS + 8, NT), block, plane, (2,) + plane, plane, plane,
                line, line, (2 * ROWS, NT), (2 * ROWS, NT), (2, 8, 128), (32, 128), (16, 128))
        ] + [
            dma((6,)), dma((4,)), dma((4,)), dma((2,)), dma((2,)), dma((2,)), dma((2,)),
            pltpu.SemaphoreType.REGULAR((3,))],
        compiler_params=pltpu.CompilerParams(
            collective_id=0, has_side_effects=True, vmem_limit_bytes=24 * 2**20),
    )(*operands)


def update_kernel(sol, res, u, image, coef, new_sol_hbm, new_res_hbm, new_dir_hbm, outs, sems):
    alpha = jnp.broadcast_to(coef[0:1, 0:128], (8, 128))
    beta = jnp.broadcast_to(coef[1:2, 0:128], (8, 128))
    alpha = jnp.concatenate([alpha] * (NT // 128), axis=1)
    beta = jnp.concatenate([beta] * (NT // 128), axis=1)
    copies = []
    for i in range(ROWS):
        def strip(jb, _, i=i):
            rows = pl.ds(pl.multiple_of(jb * 8, 8), 8)
            here = u[i, rows]
            r = res[i, rows] - alpha * image[i, rows]
            outs[0, i, rows] = sol[i, rows] + alpha * here
            outs[1, i, rows] = r
            outs[2, i, rows] = r + beta * here
            return 0
        lax.fori_loop(0, STRIPS, strip, 0, unroll=True)
        for k, target in enumerate((new_sol_hbm, new_res_hbm, new_dir_hbm)):
            copies.append(pltpu.make_async_copy(outs.at[k, i], target.at[i], sems.at[k, i]))
            copies[-1].start()
    for copy in copies:
        copy.wait()


def update(sol, res, u, image, coef):
    hbm, vmem = pl.BlockSpec(memory_space=pl.ANY), pl.BlockSpec(memory_space=pltpu.VMEM)
    block = (ROWS, COLS, NT)
    return pl.pallas_call(
        update_kernel,
        out_shape=(jax.ShapeDtypeStruct(block, F32),) * 3,
        in_specs=[vmem] * 5,
        out_specs=(hbm,) * 3,
        scratch_shapes=[pltpu.VMEM((3,) + block, F32), pltpu.SemaphoreType.DMA((3, ROWS))],
        compiler_params=pltpu.CompilerParams(vmem_limit_bytes=8 * 2**20),
    )(sol, res, u, image, coef)


def body(solution, residual, direction, slope_il, slope_xl, weights):
    return update(*apply(solution, residual, direction, slope_il, slope_xl, weights))


def solution(mesh):
    spec = P("il", "xl", None)
    return jax.shard_map(
        body, mesh=mesh, in_specs=(spec,) * 6, out_specs=(spec,) * 3, check_vma=False)
```

```python
import jax
import jax.numpy as jnp
from jax import lax
from jax.experimental import pallas as pl
from jax.experimental.pallas import tpu as pltpu
from jax.sharding import PartitionSpec as P

damping = 0.3
F32 = jnp.float32
MESH_ID = pl.DeviceIdType.MESH

NIL, NXL = 64, 8
ROWS, COLS, NT = 4, 64, 512
STRIPS = COLS // 8


def kernel(
    sol_hbm, res_hbm, u_hbm, sil_hbm, sxl_hbm, w_hbm,
    sol, res, u, image, coef,
    sil, sxl, w, fil, fx, h, u_in, w_in, g_out, g_in, xl_u_out, xl_u_in, xl_f_out, xl_f_in,
    msg, box_xy, box_zc,
    load_sem, i_send, i_recv, x_send, x_recv, r_send, r_recv, go,
):
    il, xl = lax.axis_index("il"), lax.axis_index("xl")
    z_hi, y, core = il // 16, (il // 2) % 8, il % 2
    z_lo, x = xl // 4, xl % 4
    z = z_hi * 2 + z_lo

    def at(dx=0, dy=0, dz=0, dc=0):
        nz = (z + dz) % 8
        return ((nz // 2) * 16 + ((y + dy) % 8) * 2 + (core + dc) % 2, (nz % 2) * 4 + (x + dx) % 4)

    next_il, prev_il = ((il + 1) % NIL, xl), ((il + NIL - 1) % NIL, xl)
    next_xl, prev_xl = (il, (xl + 1) % NXL), (il, (xl + NXL - 1) % NXL)
    has_next_il, has_prev_il = il < NIL - 1, il > 0
    has_next_xl, has_prev_xl = xl < NXL - 1, xl > 0
    sibling = at(dc=1)

    barrier = pltpu.get_barrier_semaphore()
    flat, deep = [at(dx=1), at(dx=3), at(dy=1), at(dy=7)], [at(dz=1), at(dz=7)]
    mesh_peers = (
        (has_next_il, next_il), (has_prev_il, prev_il), (has_next_xl, next_xl), (has_prev_xl, prev_xl))
    steps = (
        flat, [at(dy=2), at(dy=6)], [at(dx=1), at(dx=2), at(dx=3)],
        deep, [at(dz=2), at(dz=6)], [sibling],
    )
    for has, other in mesh_peers:
        @pl.when(has)
        def _(other=other):
            pl.semaphore_signal(barrier, inc=1, device_id=other, device_id_type=MESH_ID)
    for other in flat + deep:
        pl.semaphore_signal(barrier, inc=1, device_id=other, device_id_type=MESH_ID)

    def say(step):
        for other in steps[step]:
            pl.semaphore_signal(go.at[step], inc=1, device_id=other, device_id_type=MESH_ID)

    def hear(step):
        pl.semaphore_wait(go.at[step], len(steps[step]))

    loads = [
        pltpu.make_async_copy(source, target, load_sem.at[k])
        for k, (source, target) in enumerate((
            (u_hbm, u), (w_hbm, w), (sil_hbm, sil), (sxl_hbm, sxl), (res_hbm, res), (sol_hbm, sol)))
    ]
    for load in loads[:4]:
        load.start()
    count = len(flat + deep)
    for has, _ in mesh_peers:
        count = count + has.astype(jnp.int32)
    pl.semaphore_wait(barrier, count)
    say(0)
    say(3)

    i_u = pltpu.make_async_remote_copy(
        u_hbm.at[0], u_in, i_send.at[0], i_recv.at[0], prev_il, MESH_ID)
    i_w = pltpu.make_async_remote_copy(
        w_hbm.at[ROWS - 1], w_in, i_send.at[1], i_recv.at[1], next_il, MESH_ID)
    i_g = pltpu.make_async_remote_copy(g_out, g_in, i_send.at[2], i_recv.at[2], next_il, MESH_ID)
    x_u = pltpu.make_async_remote_copy(
        xl_u_out, xl_u_in, x_send.at[0], x_recv.at[0], prev_xl, MESH_ID)
    x_f = pltpu.make_async_remote_copy(
        xl_f_out, xl_f_in, x_send.at[1], x_recv.at[1], next_xl, MESH_ID)
    pl.when(has_next_il)(i_w.start)
    pl.when(has_prev_il)(i_u.start)

    lane = lax.broadcasted_iota(jnp.int32, (8, NT), 1)
    sub = lax.broadcasted_iota(jnp.int32, (8, NT), 0)
    first_t, last_t = lane == 0, lane == NT - 1
    first_r, last_r = sub == 0, sub == 7

    def diff_t(v):
        ahead = jnp.where(last_t, 0.0, pltpu.roll(v, NT - 1, 1))
        behind = jnp.where(first_t, 0.0, pltpu.roll(v, 1, 1))
        return 0.5 * (ahead - behind)

    loads[0].wait()
    loads[2].wait()

    def lean(jb, _):
        rows = pl.ds(pl.multiple_of(jb * 8, 8), 8)
        here = u[ROWS - 1, rows]
        g_out[rows] = here + sil[ROWS - 1, rows] * diff_t(here)
        return 0
    lax.fori_loop(0, STRIPS, lean, 0, unroll=True)
    pl.when(has_next_il)(i_g.start)
    loads[4].start()
    loads[5].start()

    for i in range(ROWS):
        xl_u_out[i:i + 1] = u[i, 0:1]
    pl.when(has_prev_xl)(x_u.start)
    loads[1].wait()
    loads[3].wait()
    for i in range(ROWS):
        tail = slice(COLS - 8, COLS)
        g = u[i, tail] + sxl[i, tail] * diff_t(u[i, tail])
        xl_f_out[i:i + 1] = g[7:8]
        xl_f_out[ROWS + i:ROWS + i + 1] = w[i, tail][7:8]
    pl.when(has_next_xl)(x_f.start)
    hear(0)
    say(1)
    hear(3)
    say(4)

    for has, buffers in ((has_next_il, (u_in,)), (has_prev_il, (w_in, g_in)),
                         (has_next_xl, (xl_u_in,)), (has_prev_xl, (xl_f_in,))):
        @pl.when(jnp.logical_not(has))
        def _(buffers=buffers):
            for buffer in buffers:
                buffer[...] = jnp.zeros_like(buffer)

    keep_il, keep_xl = has_next_il.astype(F32), has_next_xl.astype(F32)

    def put_strip(i, jb, next_row, last=False):
        start = pl.multiple_of(jb * 8, 8)
        rows = pl.ds(start, 8)
        here = u[i, rows]
        t = diff_t(here)
        wt = w[i, rows]
        sq = wt * wt
        ahead = jnp.where(last_r, next_row, pltpu.roll(here, 7, 0))
        slope = sxl[i, rows]
        flux = sq * (ahead - here - slope * t)
        if last:
            flux = jnp.where(last_r, keep_xl * flux, flux)
        fx[i, pl.ds(start + 8, 8)] = flux
        part = slope * flux
        if i < ROWS - 1:
            slope = sil[i, rows]
            f = sq * (u[i + 1, rows] - here - slope * t)
            fil[i, rows] = f
            part = part + slope * f
        h[i, rows] = part

    for i in range(ROWS):
        def strip(jb, _, i=i):
            put_strip(i, jb, u[i, pl.ds(jb * 8 + 8, 1)])
            return 0
        lax.fori_loop(0, STRIPS - 1, strip, 0, unroll=True)

    hear(1)
    say(2)
    hear(4)
    say(5)

    pl.when(has_next_xl)(x_u.wait_recv)
    for i in range(ROWS):
        put_strip(i, STRIPS - 1, xl_u_in[i:i + 1], True)
    pl.when(has_prev_xl)(x_f.wait_recv)
    for i in range(ROWS):
        wt = xl_f_in[ROWS + i:ROWS + i + 1]
        fx[i, 7:8] = wt * wt * (u[i, 0:1] - xl_f_in[i:i + 1])
    loads[4].wait()

    def image_strip(i, jb, sums):
        rows = pl.ds(pl.multiple_of(jb * 8, 8), 8)
        fx_here = fx[i, pl.ds(pl.multiple_of(jb * 8 + 8, 8), 8)]
        fx_behind = jnp.where(first_r, fx[i, pl.ds(jb * 8 + 7, 1)], pltpu.roll(fx_here, 1, 0))
        here = u[i, rows]
        if i == 0:
            wt = w_in[rows]
            before = wt * wt * (here - g_in[rows])
        else:
            before = fil[i - 1, rows]
        q = (before - fil[i, rows]) + (fx_behind - fx_here) + diff_t(h[i, rows]) + damping * here
        image[i, rows] = q
        r = res[i, rows]
        rr, dq, rq, qq = sums
        return rr + r * r, dq + here * q, rq + r * q, qq + q * q

    def image_inline(i, sums):
        return lax.fori_loop(0, STRIPS, lambda jb, s: image_strip(i, jb, s), sums, unroll=True)

    sums = tuple(jnp.zeros((8, NT), F32) for _ in range(4))
    for i in range(1, ROWS - 1):
        sums = image_inline(i, sums)

    pl.when(has_next_il)(i_u.wait_recv)

    def last_inline(jb, _):
        rows = pl.ds(pl.multiple_of(jb * 8, 8), 8)
        wt = w[ROWS - 1, rows]
        f = keep_il * (wt * wt * (u_in[rows] - g_out[rows]))
        fil[ROWS - 1, rows] = f
        h[ROWS - 1, rows] = h[ROWS - 1, rows] + sil[ROWS - 1, rows] * f
        return 0
    lax.fori_loop(0, STRIPS, last_inline, 0, unroll=True)
    sums = image_inline(ROWS - 1, sums)

    @pl.when(has_prev_il)
    def _():
        i_w.wait_recv()
        i_g.wait_recv()

    sums = image_inline(0, sums)
    hear(5)

    lane1 = lax.broadcasted_iota(jnp.int32, (8, 128), 1)
    row = jnp.zeros((8, 128), F32)
    for k, total in enumerate(sums):
        v = total[:, 0:128] + total[:, 128:256] + total[:, 256:384] + total[:, 384:512]
        v = v + pltpu.roll(v, 64, 1)
        v = v + pltpu.roll(v, 32, 1)
        row = jnp.where(lane1 // 32 == k, v, row)
    row = jnp.sum(row, axis=0, keepdims=True)

    near = lambda by, size: min(by, size - by)
    plane = [(dx, dy, 0, 0) for dx in range(4) for dy in range(8) if dx + dy > 0]
    plane.sort(key=lambda p: near(p[0], 4) + near(p[1], 8))
    line = [(0, 0, dz, dc) for dz in (1, 2, 3, 4, 7, 6, 5, 0) for dc in range(2) if dz + dc > 0]
    drains = []
    for phase, (offsets, box) in enumerate(((line, box_zc), (plane, box_xy))):
        count = len(offsets)
        msg[phase, 0:1] = row
        box[count:count + 1] = row
        for slot, by in enumerate(offsets):
            pltpu.make_async_remote_copy(
                msg.at[phase, pl.ds(0, 1)], box.at[pl.ds(slot, 1)],
                r_send.at[phase], r_recv.at[phase], at(*by), MESH_ID,
            ).start()
        drains.append(pltpu.make_async_remote_copy(
            box.at[pl.ds(0, count)], box.at[pl.ds(0, count)],
            r_send.at[phase], r_recv.at[phase], sibling, MESH_ID))
        drains[phase].wait_recv()
        if phase == 0:
            hear(2)
        row = jnp.sum(box[...], axis=0, keepdims=True)

    full = jnp.broadcast_to(row, (8, 128))
    rr, dq, rq, qq = (
        jnp.sum(jnp.where(lane1 // 32 == k, full, 0.0), axis=1, keepdims=True) for k in range(4))
    alpha = rr / dq
    beta = (rr - 2.0 * alpha * rq + alpha * alpha * qq) / rr
    coef[...] = jnp.where(lax.broadcasted_iota(jnp.int32, (8, 128), 0) == 0, alpha, beta)

    for has, copies in ((has_prev_il, (i_u,)), (has_next_il, (i_w, i_g)), (has_prev_xl, (x_u,)), (has_next_xl, (x_f,))):
        @pl.when(has)
        def _(copies=copies):
            for copy in copies:
                copy.wait_send()

    for drain in drains:
        drain.wait_send()
    loads[5].wait()


def apply(solution, residual, direction, slope_il, slope_xl, weights):
    hbm, vmem = pl.BlockSpec(memory_space=pltpu.HBM), pl.BlockSpec(memory_space=pltpu.VMEM)
    block, plane, line = (ROWS, COLS, NT), (COLS, NT), (ROWS, NT)
    dma = pltpu.SemaphoreType.DMA
    operands = (
        pltpu.with_memory_space_constraint(v, pltpu.HBM)
        for v in (solution, residual, direction, slope_il, slope_xl, weights))
    return pl.pallas_call(
        kernel,
        out_shape=(jax.ShapeDtypeStruct(block, F32),) * 4 + (jax.ShapeDtypeStruct((8, 128), F32),),
        in_specs=[hbm] * 6,
        out_specs=(vmem,) * 5,
        scratch_shapes=[
            pltpu.VMEM(shape, F32)
            for shape in (
                block, block, block, block, (ROWS, COLS + 8, NT), block, plane, plane, plane, plane,
                line, line, (2 * ROWS, NT), (2 * ROWS, NT), (2, 8, 128), (32, 128), (16, 128))
        ] + [
            dma((6,)), dma((3,)), dma((3,)), dma((2,)), dma((2,)), dma((2,)), dma((2,)),
            pltpu.SemaphoreType.REGULAR((6,))],
        compiler_params=pltpu.CompilerParams(
            collective_id=0, has_side_effects=True, vmem_limit_bytes=24 * 2**20),
    )(*operands)


def update_kernel(sol, res, u, image, coef, new_sol_hbm, new_res_hbm, new_dir_hbm, outs, sems):
    alpha = jnp.broadcast_to(coef[0:1, 0:128], (8, 128))
    beta = jnp.broadcast_to(coef[1:2, 0:128], (8, 128))
    alpha = jnp.concatenate([alpha] * (NT // 128), axis=1)
    beta = jnp.concatenate([beta] * (NT // 128), axis=1)
    copies = []
    for i in range(ROWS):
        def strip(jb, _, i=i):
            rows = pl.ds(pl.multiple_of(jb * 8, 8), 8)
            here = u[i, rows]
            r = res[i, rows] - alpha * image[i, rows]
            outs[0, i, rows] = sol[i, rows] + alpha * here
            outs[1, i, rows] = r
            outs[2, i, rows] = r + beta * here
            return 0
        lax.fori_loop(0, STRIPS, strip, 0, unroll=True)
        for k, target in enumerate((new_sol_hbm, new_res_hbm, new_dir_hbm)):
            copies.append(pltpu.make_async_copy(outs.at[k, i], target.at[i], sems.at[k, i]))
            copies[-1].start()
    for copy in copies:
        copy.wait()


def update(sol, res, u, image, coef):
    hbm, vmem = pl.BlockSpec(memory_space=pl.ANY), pl.BlockSpec(memory_space=pltpu.VMEM)
    block = (ROWS, COLS, NT)
    return pl.pallas_call(
        update_kernel,
        out_shape=(jax.ShapeDtypeStruct(block, F32),) * 3,
        in_specs=[vmem] * 5,
        out_specs=(hbm,) * 3,
        scratch_shapes=[pltpu.VMEM((3,) + block, F32), pltpu.SemaphoreType.DMA((3, ROWS))],
        compiler_params=pltpu.CompilerParams(vmem_limit_bytes=8 * 2**20),
    )(sol, res, u, image, coef)


def body(solution, residual, direction, slope_il, slope_xl, weights):
    return update(*apply(solution, residual, direction, slope_il, slope_xl, weights))


def solution(mesh):
    spec = P("il", "xl", None)
    return jax.shard_map(
        body, mesh=mesh, in_specs=(spec,) * 6, out_specs=(spec,) * 3, check_vma=False)
```

```python
import jax
import jax.numpy as jnp
from jax import lax
from jax.experimental import pallas as pl
from jax.experimental.pallas import tpu as pltpu
from jax.sharding import PartitionSpec as P

damping = 0.3
F32 = jnp.float32
MESH_ID = pl.DeviceIdType.MESH

NIL, NXL = 64, 8
ROWS, COLS, NT = 4, 64, 512
STRIPS = COLS // 8


def kernel(
    sol_hbm, res_hbm, u_hbm, sil_hbm, sxl_hbm, w_hbm,
    sol, res, u, image, coef,
    sil, sxl, w, fil, fx, h, u_in, w_in, g_out, g_in, st_w, st_g, xl_u_out, xl_u_in, xl_f_out, xl_f_in,
    msg, box_xy, box_zc,
    load_sem, i_send, i_recv, s_send, s_recv, x_send, x_recv, r_send, r_recv, go,
):
    il, xl = lax.axis_index("il"), lax.axis_index("xl")
    z_hi, y, core = il // 16, (il // 2) % 8, il % 2
    z_lo, x = xl // 4, xl % 4
    z = z_hi * 2 + z_lo

    def at(dx=0, dy=0, dz=0, dc=0):
        nz = (z + dz) % 8
        return ((nz // 2) * 16 + ((y + dy) % 8) * 2 + (core + dc) % 2, (nz % 2) * 4 + (x + dx) % 4)

    next_il, prev_il = ((il + 1) % NIL, xl), ((il + NIL - 1) % NIL, xl)
    next_xl, prev_xl = (il, (xl + 1) % NXL), (il, (xl + NXL - 1) % NXL)
    has_next_il, has_prev_il = il < NIL - 1, il > 0
    has_next_xl, has_prev_xl = xl < NXL - 1, xl > 0
    last_y, first_y = jnp.logical_and(y == 7, core == 1), jnp.logical_and(y == 0, core == 0)
    wrap_next = jnp.logical_and(last_y, has_next_il)
    wrap_prev = jnp.logical_and(first_y, has_prev_il)
    is_stage = jnp.logical_and(last_y, jnp.logical_and(z > 0, z < 7))
    near_next = jnp.logical_and(has_next_il, jnp.logical_not(wrap_next))
    near_prev = jnp.logical_and(has_prev_il, jnp.logical_not(wrap_prev))
    stage, my_stage, staged = at(dz=1), at(dy=7, dz=7, dc=1), at(dy=1, dz=1, dc=1)
    sibling = at(dc=1)

    barrier = pltpu.get_barrier_semaphore()
    flat, deep = [at(dx=1), at(dx=3), at(dy=1), at(dy=7)], [at(dz=1), at(dz=7)]
    mesh_peers = (
        (has_next_il, next_il), (near_prev, prev_il), (has_next_xl, next_xl), (has_prev_xl, prev_xl),
        (wrap_prev, my_stage))
    heard = (has_prev_il, near_next, has_prev_xl, has_next_xl, is_stage)
    steps = (
        flat, [at(dy=2), at(dy=6)], [at(dx=1), at(dx=2), at(dx=3)],
        deep, [at(dz=2), at(dz=6)], [sibling],
    )
    for has, other in mesh_peers:
        @pl.when(has)
        def _(other=other):
            pl.semaphore_signal(barrier, inc=1, device_id=other, device_id_type=MESH_ID)
    for other in flat + deep:
        pl.semaphore_signal(barrier, inc=1, device_id=other, device_id_type=MESH_ID)

    def say(step):
        for other in steps[step]:
            pl.semaphore_signal(go.at[step], inc=1, device_id=other, device_id_type=MESH_ID)

    def hear(step):
        pl.semaphore_wait(go.at[step], len(steps[step]))

    loads = [
        pltpu.make_async_copy(source, target, load_sem.at[k])
        for k, (source, target) in enumerate((
            (u_hbm, u), (w_hbm, w), (sil_hbm, sil), (sxl_hbm, sxl), (res_hbm, res), (sol_hbm, sol)))
    ]
    for load in loads[:4]:
        load.start()
    count = len(flat + deep)
    for has in heard:
        count = count + has.astype(jnp.int32)
    pl.semaphore_wait(barrier, count)
    say(0)
    say(3)

    i_u = pltpu.make_async_remote_copy(
        u_hbm.at[0], u_in, i_send.at[0], i_recv.at[0], prev_il, MESH_ID)
    half = COLS // 2

    def piece(k, weights, leaning):
        return (weights if k < 2 else leaning).at[pl.ds(k % 2 * half, half)]

    def copy_of(k, source, target, send_sem, recv_sem, device):
        return pltpu.make_async_remote_copy(
            piece(k, *source), piece(k, *target), send_sem, recv_sem, device, MESH_ID)

    mine, theirs, passing = (w_hbm.at[ROWS - 1], g_out), (w_in, g_in), (st_w, st_g)
    near = [copy_of(k, mine, theirs, i_send.at[1 + k], i_recv.at[1 + k], next_il) for k in range(4)]
    far = [copy_of(k, mine, passing, i_send.at[1 + k], s_recv.at[k], stage) for k in range(4)]
    relay = [copy_of(k, passing, theirs, s_send.at[k], i_recv.at[1 + k], staged) for k in range(4)]

    def send(k):
        pl.when(near_next)(near[k].start)
        pl.when(wrap_next)(far[k].start)

    def pass_on(k):
        @pl.when(is_stage)
        def _():
            far[k].wait_recv()
            relay[k].start()

    x_u = pltpu.make_async_remote_copy(
        xl_u_out, xl_u_in, x_send.at[0], x_recv.at[0], prev_xl, MESH_ID)
    x_f = pltpu.make_async_remote_copy(
        xl_f_out, xl_f_in, x_send.at[1], x_recv.at[1], next_xl, MESH_ID)
    pl.when(near_next)(near[0].start)
    send(1)
    pl.when(has_prev_il)(i_u.start)

    lane = lax.broadcasted_iota(jnp.int32, (8, NT), 1)
    sub = lax.broadcasted_iota(jnp.int32, (8, NT), 0)
    first_t, last_t = lane == 0, lane == NT - 1
    first_r, last_r = sub == 0, sub == 7

    def diff_t(v):
        ahead = jnp.where(last_t, 0.0, pltpu.roll(v, NT - 1, 1))
        behind = jnp.where(first_t, 0.0, pltpu.roll(v, 1, 1))
        return 0.5 * (ahead - behind)

    loads[0].wait()
    loads[2].wait()

    def lean(jb, _):
        rows = pl.ds(pl.multiple_of(jb * 8, 8), 8)
        here = u[ROWS - 1, rows]
        g_out[rows] = here + sil[ROWS - 1, rows] * diff_t(here)
        return 0
    lax.fori_loop(0, STRIPS // 2, lean, 0, unroll=True)
    send(2)
    lax.fori_loop(STRIPS // 2, STRIPS, lean, 0, unroll=True)
    send(3)
    loads[4].start()
    loads[5].start()

    for i in range(ROWS):
        xl_u_out[i:i + 1] = u[i, 0:1]
    pl.when(has_prev_xl)(x_u.start)
    loads[1].wait()
    loads[3].wait()
    for i in range(ROWS):
        tail = slice(COLS - 8, COLS)
        g = u[i, tail] + sxl[i, tail] * diff_t(u[i, tail])
        xl_f_out[i:i + 1] = g[7:8]
        xl_f_out[ROWS + i:ROWS + i + 1] = w[i, tail][7:8]
    pl.when(has_next_xl)(x_f.start)
    hear(0)
    say(1)
    hear(3)
    pl.when(wrap_next)(near[0].start)
    say(4)

    for has, buffers in ((has_next_il, (u_in,)), (has_prev_il, (w_in, g_in)),
                         (has_next_xl, (xl_u_in,)), (has_prev_xl, (xl_f_in,))):
        @pl.when(jnp.logical_not(has))
        def _(buffers=buffers):
            for buffer in buffers:
                buffer[...] = jnp.zeros_like(buffer)

    keep_il, keep_xl = has_next_il.astype(F32), has_next_xl.astype(F32)

    def put_strip(i, jb, next_row, last=False):
        start = pl.multiple_of(jb * 8, 8)
        rows = pl.ds(start, 8)
        here = u[i, rows]
        t = diff_t(here)
        wt = w[i, rows]
        sq = wt * wt
        ahead = jnp.where(last_r, next_row, pltpu.roll(here, 7, 0))
        slope = sxl[i, rows]
        flux = sq * (ahead - here - slope * t)
        if last:
            flux = jnp.where(last_r, keep_xl * flux, flux)
        fx[i, pl.ds(start + 8, 8)] = flux
        part = slope * flux
        if i < ROWS - 1:
            slope = sil[i, rows]
            f = sq * (u[i + 1, rows] - here - slope * t)
            fil[i, rows] = f
            part = part + slope * f
        h[i, rows] = part

    for i in range(ROWS):
        def strip(jb, _, i=i):
            put_strip(i, jb, u[i, pl.ds(jb * 8 + 8, 1)])
            return 0
        lax.fori_loop(0, STRIPS - 1, strip, 0, unroll=True)

    pass_on(1)
    hear(1)
    say(2)
    hear(4)
    say(5)
    pass_on(2)
    pass_on(3)

    pl.when(has_next_xl)(x_u.wait_recv)
    for i in range(ROWS):
        put_strip(i, STRIPS - 1, xl_u_in[i:i + 1], True)
    pl.when(has_prev_xl)(x_f.wait_recv)
    for i in range(ROWS):
        wt = xl_f_in[ROWS + i:ROWS + i + 1]
        fx[i, 7:8] = wt * wt * (u[i, 0:1] - xl_f_in[i:i + 1])
    loads[4].wait()

    def image_strip(i, jb, sums):
        rows = pl.ds(pl.multiple_of(jb * 8, 8), 8)
        fx_here = fx[i, pl.ds(pl.multiple_of(jb * 8 + 8, 8), 8)]
        fx_behind = jnp.where(first_r, fx[i, pl.ds(jb * 8 + 7, 1)], pltpu.roll(fx_here, 1, 0))
        here = u[i, rows]
        if i == 0:
            wt = w_in[rows]
            before = wt * wt * (here - g_in[rows])
        else:
            before = fil[i - 1, rows]
        q = (before - fil[i, rows]) + (fx_behind - fx_here) + diff_t(h[i, rows]) + damping * here
        image[i, rows] = q
        r = res[i, rows]
        rr, dq, rq, qq = sums
        return rr + r * r, dq + here * q, rq + r * q, qq + q * q

    def image_inline(i, sums):
        return lax.fori_loop(0, STRIPS, lambda jb, s: image_strip(i, jb, s), sums, unroll=True)

    sums = tuple(jnp.zeros((8, NT), F32) for _ in range(4))
    for i in range(1, ROWS - 1):
        sums = image_inline(i, sums)

    pl.when(has_next_il)(i_u.wait_recv)

    def last_inline(jb, _):
        rows = pl.ds(pl.multiple_of(jb * 8, 8), 8)
        wt = w[ROWS - 1, rows]
        f = keep_il * (wt * wt * (u_in[rows] - g_out[rows]))
        fil[ROWS - 1, rows] = f
        h[ROWS - 1, rows] = h[ROWS - 1, rows] + sil[ROWS - 1, rows] * f
        return 0
    lax.fori_loop(0, STRIPS, last_inline, 0, unroll=True)
    sums = image_inline(ROWS - 1, sums)

    @pl.when(has_prev_il)
    def _():
        for k in range(4):
            near[k].wait_recv()

    sums = image_inline(0, sums)
    hear(5)

    lane1 = lax.broadcasted_iota(jnp.int32, (8, 128), 1)
    row = jnp.zeros((8, 128), F32)
    for k, total in enumerate(sums):
        v = total[:, 0:128] + total[:, 128:256] + total[:, 256:384] + total[:, 384:512]
        v = v + pltpu.roll(v, 64, 1)
        v = v + pltpu.roll(v, 32, 1)
        row = jnp.where(lane1 // 32 == k, v, row)
    row = jnp.sum(row, axis=0, keepdims=True)

    hops = lambda by, size: min(by, size - by)
    plane = [(dx, dy, 0, 0) for dx in range(4) for dy in range(8) if dx + dy > 0]
    plane.sort(key=lambda p: -hops(p[0], 4) - hops(p[1], 8))
    line = [(0, 0, dz, dc) for dz in (1, 2, 3, 4, 7, 6, 5, 0) for dc in range(2) if dz + dc > 0]
    def finish():
        for has, copies in ((has_prev_il, [i_u]), (has_next_il, near), (has_prev_xl, [x_u]), (has_next_xl, [x_f]),
                            (is_stage, relay[1:])):
            @pl.when(has)
            def _(copies=copies):
                for copy in copies:
                    copy.wait_send()
        loads[5].wait()

    drains = []
    for phase, (offsets, box) in enumerate(((line, box_zc), (plane, box_xy))):
        count = len(offsets)
        msg[phase, 0:1] = row
        box[count:count + 1] = row
        for slot, by in enumerate(offsets):
            pltpu.make_async_remote_copy(
                msg.at[phase, pl.ds(0, 1)], box.at[pl.ds(slot, 1)],
                r_send.at[phase], r_recv.at[phase], at(*by), MESH_ID,
            ).start()
        drains.append(pltpu.make_async_remote_copy(
            box.at[pl.ds(0, count)], box.at[pl.ds(0, count)],
            r_send.at[phase], r_recv.at[phase], sibling, MESH_ID))
        drains[phase].wait_send()
        if phase == 1:
            finish()
        drains[phase].wait_recv()
        if phase == 0:
            hear(2)
        row = jnp.sum(box[...], axis=0, keepdims=True)

    full = jnp.broadcast_to(row, (8, 128))
    rr, dq, rq, qq = (
        jnp.sum(jnp.where(lane1 // 32 == k, full, 0.0), axis=1, keepdims=True) for k in range(4))
    alpha = rr / dq
    beta = (rr - 2.0 * alpha * rq + alpha * alpha * qq) / rr
    coef[...] = jnp.where(lax.broadcasted_iota(jnp.int32, (8, 128), 0) == 0, alpha, beta)


def apply(solution, residual, direction, slope_il, slope_xl, weights):
    hbm, vmem = pl.BlockSpec(memory_space=pltpu.HBM), pl.BlockSpec(memory_space=pltpu.VMEM)
    block, plane, line = (ROWS, COLS, NT), (COLS, NT), (ROWS, NT)
    dma = pltpu.SemaphoreType.DMA
    operands = (
        pltpu.with_memory_space_constraint(v, pltpu.HBM)
        for v in (solution, residual, direction, slope_il, slope_xl, weights))
    return pl.pallas_call(
        kernel,
        out_shape=(jax.ShapeDtypeStruct(block, F32),) * 4 + (jax.ShapeDtypeStruct((8, 128), F32),),
        in_specs=[hbm] * 6,
        out_specs=(vmem,) * 5,
        scratch_shapes=[
            pltpu.VMEM(shape, F32)
            for shape in (
                block, block, block, block, (ROWS, COLS + 8, NT), block, plane, plane, plane, plane, plane, plane,
                line, line, (2 * ROWS, NT), (2 * ROWS, NT), (2, 8, 128), (32, 128), (16, 128))
        ] + [
            dma((6,)), dma((5,)), dma((5,)), dma((4,)), dma((4,)), dma((2,)), dma((2,)), dma((2,)), dma((2,)),
            pltpu.SemaphoreType.REGULAR((6,))],
        compiler_params=pltpu.CompilerParams(
            collective_id=0, has_side_effects=True, vmem_limit_bytes=24 * 2**20),
    )(*operands)


def update_kernel(sol, res, u, image, coef, new_sol_hbm, new_res_hbm, new_dir_hbm, outs, sems):
    alpha = jnp.broadcast_to(coef[0:1, 0:128], (8, 128))
    beta = jnp.broadcast_to(coef[1:2, 0:128], (8, 128))
    alpha = jnp.concatenate([alpha] * (NT // 128), axis=1)
    beta = jnp.concatenate([beta] * (NT // 128), axis=1)
    copies = []
    for i in range(ROWS):
        def strip(jb, _, i=i):
            rows = pl.ds(pl.multiple_of(jb * 8, 8), 8)
            here = u[i, rows]
            r = res[i, rows] - alpha * image[i, rows]
            outs[0, i, rows] = sol[i, rows] + alpha * here
            outs[1, i, rows] = r
            outs[2, i, rows] = r + beta * here
            return 0
        lax.fori_loop(0, STRIPS, strip, 0, unroll=True)
        for k, target in enumerate((new_sol_hbm, new_res_hbm, new_dir_hbm)):
            copies.append(pltpu.make_async_copy(outs.at[k, i], target.at[i], sems.at[k, i]))
            copies[-1].start()
    for copy in copies:
        copy.wait()


def update(sol, res, u, image, coef):
    hbm, vmem = pl.BlockSpec(memory_space=pl.ANY), pl.BlockSpec(memory_space=pltpu.VMEM)
    block = (ROWS, COLS, NT)
    return pl.pallas_call(
        update_kernel,
        out_shape=(jax.ShapeDtypeStruct(block, F32),) * 3,
        in_specs=[vmem] * 5,
        out_specs=(hbm,) * 3,
        scratch_shapes=[pltpu.VMEM((3,) + block, F32), pltpu.SemaphoreType.DMA((3, ROWS))],
        compiler_params=pltpu.CompilerParams(vmem_limit_bytes=8 * 2**20),
    )(sol, res, u, image, coef)


def body(solution, residual, direction, slope_il, slope_xl, weights):
    return update(*apply(solution, residual, direction, slope_il, slope_xl, weights))


def solution(mesh):
    spec = P("il", "xl", None)
    return jax.shard_map(
        body, mesh=mesh, in_specs=(spec,) * 6, out_specs=(spec,) * 3, check_vma=False)
```

```python
import jax
import jax.numpy as jnp
from jax import lax
from jax.experimental import pallas as pl
from jax.experimental.pallas import tpu as pltpu
from jax.sharding import PartitionSpec as P

damping = 0.3
F32 = jnp.float32
MESH_ID = pl.DeviceIdType.MESH

NIL, NXL = 64, 8
ROWS, COLS, NT = 4, 64, 512
STRIPS = COLS // 8


def kernel(
    sol_hbm, res_hbm, u_hbm, sil_hbm, sxl_hbm, w_hbm,
    sol, res, u, image, coef,
    sil, sxl, w, fil, fx, h, u_in, w_in, g_out, g_in, st_w, st_g, xl_u_out, xl_u_in, xl_f_out, xl_f_in,
    msg, box_xy, box_zc,
    load_sem, i_send, i_recv, s_send, s_recv, x_send, x_recv, r_send, r_recv, go,
):
    loads = [
        pltpu.make_async_copy(source, target, load_sem.at[k])
        for k, (source, target) in enumerate((
            (u_hbm, u), (w_hbm, w), (sil_hbm, sil), (sxl_hbm, sxl), (res_hbm, res), (sol_hbm, sol)))
    ]
    for load in loads[:4]:
        load.start()
    il, xl = lax.axis_index("il"), lax.axis_index("xl")
    z_hi, y, core = il // 16, (il // 2) % 8, il % 2
    z_lo, x = xl // 4, xl % 4
    z = z_hi * 2 + z_lo

    def at(dx=0, dy=0, dz=0, dc=0):
        nz = (z + dz) % 8
        return ((nz // 2) * 16 + ((y + dy) % 8) * 2 + (core + dc) % 2, (nz % 2) * 4 + (x + dx) % 4)

    next_il, prev_il = ((il + 1) % NIL, xl), ((il + NIL - 1) % NIL, xl)
    next_xl, prev_xl = (il, (xl + 1) % NXL), (il, (xl + NXL - 1) % NXL)
    has_next_il, has_prev_il = il < NIL - 1, il > 0
    has_next_xl, has_prev_xl = xl < NXL - 1, xl > 0
    last_y, first_y = jnp.logical_and(y == 7, core == 1), jnp.logical_and(y == 0, core == 0)
    wrap_next = jnp.logical_and(last_y, has_next_il)
    wrap_prev = jnp.logical_and(first_y, has_prev_il)
    is_stage = jnp.logical_and(last_y, jnp.logical_and(z > 0, z < 7))
    near_next = jnp.logical_and(has_next_il, jnp.logical_not(wrap_next))
    near_prev = jnp.logical_and(has_prev_il, jnp.logical_not(wrap_prev))
    stage, my_stage, staged = at(dz=1), at(dy=7, dz=7, dc=1), at(dy=1, dz=1, dc=1)
    sibling = at(dc=1)

    barrier = pltpu.get_barrier_semaphore()
    flat, deep = [at(dx=1), at(dx=3), at(dy=1), at(dy=7)], [at(dz=1), at(dz=7)]
    mesh_peers = (
        (has_next_il, next_il), (near_prev, prev_il), (has_next_xl, next_xl), (has_prev_xl, prev_xl),
        (wrap_prev, my_stage))
    heard = (has_prev_il, near_next, has_prev_xl, has_next_xl, is_stage)
    steps = (
        flat, [at(dy=2), at(dy=6)], [at(dx=1), at(dx=2), at(dx=3)],
        deep, [at(dz=2), at(dz=6)], [sibling],
    )
    for has, other in mesh_peers:
        @pl.when(has)
        def _(other=other):
            pl.semaphore_signal(barrier, inc=1, device_id=other, device_id_type=MESH_ID)
    for other in flat + deep:
        pl.semaphore_signal(barrier, inc=1, device_id=other, device_id_type=MESH_ID)

    def say(step):
        for other in steps[step]:
            pl.semaphore_signal(go.at[step], inc=1, device_id=other, device_id_type=MESH_ID)

    def hear(step):
        pl.semaphore_wait(go.at[step], len(steps[step]))

    count = len(flat + deep)
    for has in heard:
        count = count + has.astype(jnp.int32)
    pl.semaphore_wait(barrier, count)
    say(0)
    say(3)

    i_u = pltpu.make_async_remote_copy(
        u.at[0], u_in, i_send.at[0], i_recv.at[0], prev_il, MESH_ID)
    half = COLS // 2

    def piece(k, weights, leaning):
        return (weights if k < 2 else leaning).at[pl.ds(k % 2 * half, half)]

    def copy_of(k, source, target, send_sem, recv_sem, device):
        return pltpu.make_async_remote_copy(
            piece(k, *source), piece(k, *target), send_sem, recv_sem, device, MESH_ID)

    mine, theirs, passing = (w.at[ROWS - 1], g_out), (w_in, g_in), (st_w, st_g)
    near = [copy_of(k, mine, theirs, i_send.at[1 + k], i_recv.at[1 + k], next_il) for k in range(4)]
    far = [copy_of(k, mine, passing, i_send.at[1 + k], s_recv.at[k], stage) for k in range(4)]
    relay = [copy_of(k, passing, theirs, s_send.at[k], i_recv.at[1 + k], staged) for k in range(4)]

    def send(k):
        pl.when(near_next)(near[k].start)
        pl.when(wrap_next)(far[k].start)

    def pass_on(k):
        @pl.when(is_stage)
        def _():
            far[k].wait_recv()
            relay[k].start()

    x_u = pltpu.make_async_remote_copy(
        xl_u_out, xl_u_in, x_send.at[0], x_recv.at[0], prev_xl, MESH_ID)
    x_f = pltpu.make_async_remote_copy(
        xl_f_out, xl_f_in, x_send.at[1], x_recv.at[1], next_xl, MESH_ID)
    loads[0].wait()
    pl.when(has_prev_il)(i_u.start)
    loads[1].wait()
    pl.when(near_next)(near[0].start)
    send(1)

    lane = lax.broadcasted_iota(jnp.int32, (8, NT), 1)
    sub = lax.broadcasted_iota(jnp.int32, (8, NT), 0)
    first_t, last_t = lane == 0, lane == NT - 1
    first_r, last_r = sub == 0, sub == 7

    def diff_t(v):
        ahead = jnp.where(last_t, 0.0, pltpu.roll(v, NT - 1, 1))
        behind = jnp.where(first_t, 0.0, pltpu.roll(v, 1, 1))
        return 0.5 * (ahead - behind)

    loads[2].wait()

    def lean(jb, _):
        rows = pl.ds(pl.multiple_of(jb * 8, 8), 8)
        here = u[ROWS - 1, rows]
        g_out[rows] = here + sil[ROWS - 1, rows] * diff_t(here)
        return 0
    lax.fori_loop(0, STRIPS // 2, lean, 0, unroll=True)
    send(2)
    lax.fori_loop(STRIPS // 2, STRIPS, lean, 0, unroll=True)
    send(3)
    loads[4].start()
    loads[5].start()

    for i in range(ROWS):
        xl_u_out[i:i + 1] = u[i, 0:1]
    pl.when(has_prev_xl)(x_u.start)
    loads[3].wait()
    for i in range(ROWS):
        tail = slice(COLS - 8, COLS)
        g = u[i, tail] + sxl[i, tail] * diff_t(u[i, tail])
        xl_f_out[i:i + 1] = g[7:8]
        xl_f_out[ROWS + i:ROWS + i + 1] = w[i, tail][7:8]
    pl.when(has_next_xl)(x_f.start)
    hear(0)
    say(1)
    hear(3)
    pl.when(wrap_next)(near[0].start)
    say(4)

    for has, buffers in ((has_next_il, (u_in,)), (has_prev_il, (w_in, g_in)),
                         (has_next_xl, (xl_u_in,)), (has_prev_xl, (xl_f_in,))):
        @pl.when(jnp.logical_not(has))
        def _(buffers=buffers):
            for buffer in buffers:
                buffer[...] = jnp.zeros_like(buffer)

    keep_il, keep_xl = has_next_il.astype(F32), has_next_xl.astype(F32)

    def put_strip(i, jb, next_row, last=False):
        start = pl.multiple_of(jb * 8, 8)
        rows = pl.ds(start, 8)
        here = u[i, rows]
        t = diff_t(here)
        wt = w[i, rows]
        sq = wt * wt
        ahead = jnp.where(last_r, next_row, pltpu.roll(here, 7, 0))
        slope = sxl[i, rows]
        flux = sq * (ahead - here - slope * t)
        if last:
            flux = jnp.where(last_r, keep_xl * flux, flux)
        fx[i, pl.ds(start + 8, 8)] = flux
        part = slope * flux
        if i < ROWS - 1:
            slope = sil[i, rows]
            f = sq * (u[i + 1, rows] - here - slope * t)
            fil[i, rows] = f
            part = part + slope * f
        h[i, rows] = part

    for i in range(ROWS):
        def strip(jb, _, i=i):
            put_strip(i, jb, u[i, pl.ds(jb * 8 + 8, 1)])
            return 0
        lax.fori_loop(0, STRIPS - 1, strip, 0, unroll=True)

    pass_on(1)
    hear(1)
    say(2)
    hear(4)
    say(5)
    pass_on(2)
    pass_on(3)

    pl.when(has_next_xl)(x_u.wait_recv)
    for i in range(ROWS):
        put_strip(i, STRIPS - 1, xl_u_in[i:i + 1], True)
    pl.when(has_prev_xl)(x_f.wait_recv)
    for i in range(ROWS):
        wt = xl_f_in[ROWS + i:ROWS + i + 1]
        fx[i, 7:8] = wt * wt * (u[i, 0:1] - xl_f_in[i:i + 1])
    loads[4].wait()

    def image_strip(i, jb, sums):
        rows = pl.ds(pl.multiple_of(jb * 8, 8), 8)
        fx_here = fx[i, pl.ds(pl.multiple_of(jb * 8 + 8, 8), 8)]
        fx_behind = jnp.where(first_r, fx[i, pl.ds(jb * 8 + 7, 1)], pltpu.roll(fx_here, 1, 0))
        here = u[i, rows]
        if i == 0:
            wt = w_in[rows]
            before = wt * wt * (here - g_in[rows])
        else:
            before = fil[i - 1, rows]
        q = (before - fil[i, rows]) + (fx_behind - fx_here) + diff_t(h[i, rows]) + damping * here
        image[i, rows] = q
        r = res[i, rows]
        rr, dq, rq, qq = sums
        return rr + r * r, dq + here * q, rq + r * q, qq + q * q

    def image_inline(i, sums):
        return lax.fori_loop(0, STRIPS, lambda jb, s: image_strip(i, jb, s), sums, unroll=True)

    sums = tuple(jnp.zeros((8, NT), F32) for _ in range(4))
    for i in range(1, ROWS - 1):
        sums = image_inline(i, sums)

    pl.when(has_next_il)(i_u.wait_recv)

    def last_inline(jb, _):
        rows = pl.ds(pl.multiple_of(jb * 8, 8), 8)
        wt = w[ROWS - 1, rows]
        f = keep_il * (wt * wt * (u_in[rows] - g_out[rows]))
        fil[ROWS - 1, rows] = f
        h[ROWS - 1, rows] = h[ROWS - 1, rows] + sil[ROWS - 1, rows] * f
        return 0
    lax.fori_loop(0, STRIPS, last_inline, 0, unroll=True)
    sums = image_inline(ROWS - 1, sums)

    @pl.when(has_prev_il)
    def _():
        for k in range(4):
            near[k].wait_recv()

    sums = image_inline(0, sums)
    hear(5)

    lane1 = lax.broadcasted_iota(jnp.int32, (8, 128), 1)
    row = jnp.zeros((8, 128), F32)
    for k, total in enumerate(sums):
        v = total[:, 0:128] + total[:, 128:256] + total[:, 256:384] + total[:, 384:512]
        v = v + pltpu.roll(v, 64, 1)
        v = v + pltpu.roll(v, 32, 1)
        row = jnp.where(lane1 // 32 == k, v, row)
    row = jnp.sum(row, axis=0, keepdims=True)

    hops = lambda by, size: min(by, size - by)
    plane = [(dx, dy, 0, 0) for dx in range(4) for dy in range(8) if dx + dy > 0]
    plane.sort(key=lambda p: -hops(p[0], 4) - hops(p[1], 8))
    line = [(0, 0, dz, dc) for dz in (1, 2, 3, 4, 7, 6, 5, 0) for dc in range(2) if dz + dc > 0]
    def finish():
        for has, copies in ((has_prev_il, [i_u]), (has_next_il, near), (has_prev_xl, [x_u]), (has_next_xl, [x_f]),
                            (is_stage, relay[1:])):
            @pl.when(has)
            def _(copies=copies):
                for copy in copies:
                    copy.wait_send()
        loads[5].wait()

    drains = []
    for phase, (offsets, box) in enumerate(((line, box_zc), (plane, box_xy))):
        count = len(offsets)
        msg[phase, 0:1] = row
        box[count:count + 1] = row
        for slot, by in enumerate(offsets):
            pltpu.make_async_remote_copy(
                msg.at[phase, pl.ds(0, 1)], box.at[pl.ds(slot, 1)],
                r_send.at[phase], r_recv.at[phase], at(*by), MESH_ID,
            ).start()
        drains.append(pltpu.make_async_remote_copy(
            box.at[pl.ds(0, count)], box.at[pl.ds(0, count)],
            r_send.at[phase], r_recv.at[phase], sibling, MESH_ID))
        drains[phase].wait_send()
        if phase == 1:
            finish()
        drains[phase].wait_recv()
        if phase == 0:
            hear(2)
        row = jnp.sum(box[...], axis=0, keepdims=True)

    full = jnp.broadcast_to(row, (8, 128))
    rr, dq, rq, qq = (
        jnp.sum(jnp.where(lane1 // 32 == k, full, 0.0), axis=1, keepdims=True) for k in range(4))
    alpha = rr / dq
    beta = (rr - 2.0 * alpha * rq + alpha * alpha * qq) / rr
    coef[...] = jnp.where(lax.broadcasted_iota(jnp.int32, (8, 128), 0) == 0, alpha, beta)


def apply(solution, residual, direction, slope_il, slope_xl, weights):
    hbm, vmem = pl.BlockSpec(memory_space=pltpu.HBM), pl.BlockSpec(memory_space=pltpu.VMEM)
    block, plane, line = (ROWS, COLS, NT), (COLS, NT), (ROWS, NT)
    dma = pltpu.SemaphoreType.DMA
    operands = (
        pltpu.with_memory_space_constraint(v, pltpu.HBM)
        for v in (solution, residual, direction, slope_il, slope_xl, weights))
    return pl.pallas_call(
        kernel,
        out_shape=(jax.ShapeDtypeStruct(block, F32),) * 4 + (jax.ShapeDtypeStruct((8, 128), F32),),
        in_specs=[hbm] * 6,
        out_specs=(vmem,) * 5,
        scratch_shapes=[
            pltpu.VMEM(shape, F32)
            for shape in (
                block, block, block, block, (ROWS, COLS + 8, NT), block, plane, plane, plane, plane, plane, plane,
                line, line, (2 * ROWS, NT), (2 * ROWS, NT), (2, 8, 128), (32, 128), (16, 128))
        ] + [
            dma((6,)), dma((5,)), dma((5,)), dma((4,)), dma((4,)), dma((2,)), dma((2,)), dma((2,)), dma((2,)),
            pltpu.SemaphoreType.REGULAR((6,))],
        compiler_params=pltpu.CompilerParams(
            collective_id=0, has_side_effects=True, vmem_limit_bytes=24 * 2**20),
    )(*operands)


def update_kernel(sol, res, u, image, coef, new_sol_hbm, new_res_hbm, new_dir_hbm, outs, sems):
    alpha = jnp.broadcast_to(coef[0:1, 0:128], (8, 128))
    beta = jnp.broadcast_to(coef[1:2, 0:128], (8, 128))
    alpha = jnp.concatenate([alpha] * (NT // 128), axis=1)
    beta = jnp.concatenate([beta] * (NT // 128), axis=1)
    copies = []
    for i in range(ROWS):
        def strip(jb, _, i=i):
            rows = pl.ds(pl.multiple_of(jb * 8, 8), 8)
            here = u[i, rows]
            r = res[i, rows] - alpha * image[i, rows]
            outs[0, i, rows] = sol[i, rows] + alpha * here
            outs[1, i, rows] = r
            outs[2, i, rows] = r + beta * here
            return 0
        lax.fori_loop(0, STRIPS, strip, 0, unroll=True)
        for k, target in enumerate((new_sol_hbm, new_res_hbm, new_dir_hbm)):
            copies.append(pltpu.make_async_copy(outs.at[k, i], target.at[i], sems.at[k, i]))
            copies[-1].start()
    for copy in copies:
        copy.wait()


def update(sol, res, u, image, coef):
    hbm, vmem = pl.BlockSpec(memory_space=pl.ANY), pl.BlockSpec(memory_space=pltpu.VMEM)
    block = (ROWS, COLS, NT)
    return pl.pallas_call(
        update_kernel,
        out_shape=(jax.ShapeDtypeStruct(block, F32),) * 3,
        in_specs=[vmem] * 5,
        out_specs=(hbm,) * 3,
        scratch_shapes=[pltpu.VMEM((3,) + block, F32), pltpu.SemaphoreType.DMA((3, ROWS))],
        compiler_params=pltpu.CompilerParams(vmem_limit_bytes=8 * 2**20),
    )(sol, res, u, image, coef)


def body(solution, residual, direction, slope_il, slope_xl, weights):
    return update(*apply(solution, residual, direction, slope_il, slope_xl, weights))


def solution(mesh):
    spec = P("il", "xl", None)
    return jax.shard_map(
        body, mesh=mesh, in_specs=(spec,) * 6, out_specs=(spec,) * 3, check_vma=False)
```

```python
import jax
import jax.numpy as jnp
from jax import lax
from jax.experimental import pallas as pl
from jax.experimental.pallas import tpu as pltpu
from jax.sharding import PartitionSpec as P

damping = 0.3
F32 = jnp.float32
MESH_ID = pl.DeviceIdType.MESH

NIL, NXL = 64, 8
ROWS, COLS, NT = 4, 64, 512
STRIPS = COLS // 8


def kernel(
    sol_hbm, res_hbm, u_hbm, sil_hbm, sxl_hbm, w_hbm,
    sol, res, u, image, coef,
    sil, sxl, w, fil, fx, h, u_in, w_in, g_out, g_in, st_w, st_g, xl_u_out, xl_u_in, xl_f_out, xl_f_in,
    msg, box_xy, box_zc,
    load_sem, i_send, i_recv, s_send, s_recv, x_send, x_recv, r_send, r_recv, go,
):
    loads = [
        pltpu.make_async_copy(source, target, load_sem.at[k])
        for k, (source, target) in enumerate((
            (u_hbm, u), (w_hbm, w), (sil_hbm, sil), (sxl_hbm, sxl), (res_hbm, res), (sol_hbm, sol)))
    ]
    for load in loads[:4]:
        load.start()
    il, xl = lax.axis_index("il"), lax.axis_index("xl")
    z_hi, y, core = il // 16, (il // 2) % 8, il % 2
    z_lo, x = xl // 4, xl % 4
    z = z_hi * 2 + z_lo

    def at(dx=0, dy=0, dz=0, dc=0):
        nz = (z + dz) % 8
        return ((nz // 2) * 16 + ((y + dy) % 8) * 2 + (core + dc) % 2, (nz % 2) * 4 + (x + dx) % 4)

    next_il, prev_il = ((il + 1) % NIL, xl), ((il + NIL - 1) % NIL, xl)
    next_xl, prev_xl = (il, (xl + 1) % NXL), (il, (xl + NXL - 1) % NXL)
    has_next_il, has_prev_il = il < NIL - 1, il > 0
    has_next_xl, has_prev_xl = xl < NXL - 1, xl > 0
    last_y, first_y = jnp.logical_and(y == 7, core == 1), jnp.logical_and(y == 0, core == 0)
    wrap_next = jnp.logical_and(last_y, has_next_il)
    wrap_prev = jnp.logical_and(first_y, has_prev_il)
    is_stage = jnp.logical_and(last_y, jnp.logical_and(z > 0, z < 7))
    near_next = jnp.logical_and(has_next_il, jnp.logical_not(wrap_next))
    near_prev = jnp.logical_and(has_prev_il, jnp.logical_not(wrap_prev))
    stage, my_stage, staged = at(dz=1), at(dy=7, dz=7, dc=1), at(dy=1, dz=1, dc=1)
    sibling = at(dc=1)

    barrier = pltpu.get_barrier_semaphore()
    flat, deep = [at(dx=1), at(dx=3), at(dy=1), at(dy=7)], [at(dz=1), at(dz=7)]
    mesh_peers = (
        (has_next_il, next_il), (near_prev, prev_il), (has_next_xl, next_xl), (has_prev_xl, prev_xl),
        (wrap_prev, my_stage))
    heard = (has_prev_il, near_next, has_prev_xl, has_next_xl, is_stage)
    steps = (
        flat, [at(dy=2), at(dy=6)], [at(dx=1), at(dx=2), at(dx=3)],
        deep, [at(dz=2), at(dz=6)], [sibling],
    )
    for has, other in mesh_peers:
        @pl.when(has)
        def _(other=other):
            pl.semaphore_signal(barrier, inc=1, device_id=other, device_id_type=MESH_ID)
    for other in flat + deep:
        pl.semaphore_signal(barrier, inc=1, device_id=other, device_id_type=MESH_ID)

    def say(step):
        for other in steps[step]:
            pl.semaphore_signal(go.at[step], inc=1, device_id=other, device_id_type=MESH_ID)

    def hear(step):
        pl.semaphore_wait(go.at[step], len(steps[step]))

    count = len(flat + deep)
    for has in heard:
        count = count + has.astype(jnp.int32)
    pl.semaphore_wait(barrier, count)
    say(0)
    say(3)

    i_u = pltpu.make_async_remote_copy(
        u.at[0], u_in, i_send.at[0], i_recv.at[0], prev_il, MESH_ID)
    half = COLS // 2

    def piece(k, weights, leaning):
        return (weights if k < 2 else leaning).at[pl.ds(k % 2 * half, half)]

    def copy_of(k, source, target, send_sem, recv_sem, device):
        return pltpu.make_async_remote_copy(
            piece(k, *source), piece(k, *target), send_sem, recv_sem, device, MESH_ID)

    mine, theirs, passing = (w.at[ROWS - 1], g_out), (w_in, g_in), (st_w, st_g)
    near = [copy_of(k, mine, theirs, i_send.at[1 + k], i_recv.at[1 + k], next_il) for k in range(4)]
    far = [copy_of(k, mine, passing, i_send.at[1 + k], s_recv.at[k], stage) for k in range(4)]
    relay = [copy_of(k, passing, theirs, s_send.at[k], i_recv.at[1 + k], staged) for k in range(4)]

    def send(k):
        pl.when(near_next)(near[k].start)
        pl.when(wrap_next)(far[k].start)

    def pass_on(k):
        @pl.when(is_stage)
        def _():
            far[k].wait_recv()
            relay[k].start()

    x_u = pltpu.make_async_remote_copy(
        xl_u_out, xl_u_in, x_send.at[0], x_recv.at[0], prev_xl, MESH_ID)
    x_f = pltpu.make_async_remote_copy(
        xl_f_out, xl_f_in, x_send.at[1], x_recv.at[1], next_xl, MESH_ID)
    loads[0].wait()
    pl.when(has_prev_il)(i_u.start)
    loads[1].wait()
    pl.when(near_next)(near[0].start)
    send(1)

    lane = lax.broadcasted_iota(jnp.int32, (8, NT), 1)
    sub = lax.broadcasted_iota(jnp.int32, (8, NT), 0)
    first_t, last_t = lane == 0, lane == NT - 1
    first_r, last_r = sub == 0, sub == 7

    def diff_t(v):
        ahead = jnp.where(last_t, 0.0, pltpu.roll(v, NT - 1, 1))
        behind = jnp.where(first_t, 0.0, pltpu.roll(v, 1, 1))
        return 0.5 * (ahead - behind)

    loads[2].wait()

    def lean(jb, _):
        rows = pl.ds(pl.multiple_of(jb * 8, 8), 8)
        here = u[ROWS - 1, rows]
        g_out[rows] = here + sil[ROWS - 1, rows] * diff_t(here)
        return 0
    lax.fori_loop(0, STRIPS // 2, lean, 0, unroll=True)
    send(2)
    lax.fori_loop(STRIPS // 2, STRIPS, lean, 0, unroll=True)
    send(3)
    loads[4].start()
    loads[5].start()

    for i in range(ROWS):
        xl_u_out[i:i + 1] = u[i, 0:1]
    pl.when(has_prev_xl)(x_u.start)
    loads[3].wait()
    for i in range(ROWS):
        tail = slice(COLS - 8, COLS)
        g = u[i, tail] + sxl[i, tail] * diff_t(u[i, tail])
        xl_f_out[i:i + 1] = g[7:8]
        xl_f_out[ROWS + i:ROWS + i + 1] = w[i, tail][7:8]
    pl.when(has_next_xl)(x_f.start)
    hear(0)
    say(1)
    hear(3)
    pl.when(wrap_next)(near[0].start)
    say(4)

    for has, buffers in ((has_next_il, (u_in,)), (has_prev_il, (w_in, g_in)),
                         (has_next_xl, (xl_u_in,)), (has_prev_xl, (xl_f_in,))):
        @pl.when(jnp.logical_not(has))
        def _(buffers=buffers):
            for buffer in buffers:
                buffer[...] = jnp.zeros_like(buffer)

    keep_il, keep_xl = has_next_il.astype(F32), has_next_xl.astype(F32)

    def put_strip(i, jb, next_row, last=False):
        start = pl.multiple_of(jb * 8, 8)
        rows = pl.ds(start, 8)
        here = u[i, rows]
        t = diff_t(here)
        wt = w[i, rows]
        sq = wt * wt
        ahead = jnp.where(last_r, next_row, pltpu.roll(here, 7, 0))
        slope = sxl[i, rows]
        flux = sq * (ahead - here - slope * t)
        if last:
            flux = jnp.where(last_r, keep_xl * flux, flux)
        fx[i, pl.ds(start + 8, 8)] = flux
        part = slope * flux
        if i < ROWS - 1:
            slope = sil[i, rows]
            f = sq * (u[i + 1, rows] - here - slope * t)
            fil[i, rows] = f
            part = part + slope * f
        h[i, rows] = part

    for i in range(ROWS):
        def strip(jb, _, i=i):
            put_strip(i, jb, u[i, pl.ds(jb * 8 + 8, 1)])
            return 0
        lax.fori_loop(0, STRIPS - 1, strip, 0, unroll=True)

    pass_on(1)
    hear(1)
    say(2)
    hear(4)
    say(5)
    pass_on(2)
    pass_on(3)

    pl.when(has_next_xl)(x_u.wait_recv)
    for i in range(ROWS):
        put_strip(i, STRIPS - 1, xl_u_in[i:i + 1], True)
    pl.when(has_prev_xl)(x_f.wait_recv)
    for i in range(ROWS):
        wt = xl_f_in[ROWS + i:ROWS + i + 1]
        fx[i, 7:8] = wt * wt * (u[i, 0:1] - xl_f_in[i:i + 1])
    loads[4].wait()

    def image_strip(i, jb, sums):
        rows = pl.ds(pl.multiple_of(jb * 8, 8), 8)
        fx_here = fx[i, pl.ds(pl.multiple_of(jb * 8 + 8, 8), 8)]
        fx_behind = jnp.where(first_r, fx[i, pl.ds(jb * 8 + 7, 1)], pltpu.roll(fx_here, 1, 0))
        here = u[i, rows]
        if i == 0:
            wt = w_in[rows]
            before = wt * wt * (here - g_in[rows])
        else:
            before = fil[i - 1, rows]
        q = (before - fil[i, rows]) + (fx_behind - fx_here) + diff_t(h[i, rows]) + damping * here
        image[i, rows] = q
        r = res[i, rows]
        rr, dq, rq, qq = sums
        return rr + r * r, dq + here * q, rq + r * q, qq + q * q

    def image_inline(i, sums, start=0, stop=STRIPS):
        return lax.fori_loop(start, stop, lambda jb, s: image_strip(i, jb, s), sums, unroll=True)

    sums = tuple(jnp.zeros((8, NT), F32) for _ in range(4))
    for i in range(1, ROWS - 1):
        sums = image_inline(i, sums)

    pl.when(has_next_il)(i_u.wait_recv)

    def last_inline(jb, _):
        rows = pl.ds(pl.multiple_of(jb * 8, 8), 8)
        wt = w[ROWS - 1, rows]
        f = keep_il * (wt * wt * (u_in[rows] - g_out[rows]))
        fil[ROWS - 1, rows] = f
        h[ROWS - 1, rows] = h[ROWS - 1, rows] + sil[ROWS - 1, rows] * f
        return 0
    lax.fori_loop(0, STRIPS, last_inline, 0, unroll=True)
    sums = image_inline(ROWS - 1, sums)

    for part in range(2):
        @pl.when(has_prev_il)
        def _(part=part):
            near[part].wait_recv()
            near[2 + part].wait_recv()

        sums = image_inline(0, sums, part * STRIPS // 2, (part + 1) * STRIPS // 2)
    hear(5)

    lane1 = lax.broadcasted_iota(jnp.int32, (8, 128), 1)
    row = jnp.zeros((8, 128), F32)
    for k, total in enumerate(sums):
        v = total[:, 0:128] + total[:, 128:256] + total[:, 256:384] + total[:, 384:512]
        v = v + pltpu.roll(v, 64, 1)
        v = v + pltpu.roll(v, 32, 1)
        row = jnp.where(lane1 // 32 == k, v, row)
    row = jnp.sum(row, axis=0, keepdims=True)

    hops = lambda by, size: min(by, size - by)
    plane = [(dx, dy, 0, 0) for dx in range(4) for dy in range(8) if dx + dy > 0]
    plane.sort(key=lambda p: -hops(p[0], 4) - hops(p[1], 8))
    line = [(0, 0, dz, dc) for dz in (1, 2, 3, 4, 7, 6, 5, 0) for dc in range(2) if dz + dc > 0]
    def finish():
        for has, copies in ((has_prev_il, [i_u]), (has_next_il, near), (has_prev_xl, [x_u]), (has_next_xl, [x_f]),
                            (is_stage, relay[1:])):
            @pl.when(has)
            def _(copies=copies):
                for copy in copies:
                    copy.wait_send()
        loads[5].wait()

    drains = []
    for phase, (offsets, box) in enumerate(((line, box_zc), (plane, box_xy))):
        count = len(offsets)
        msg[phase, 0:1] = row
        box[count:count + 1] = row
        for slot, by in enumerate(offsets):
            pltpu.make_async_remote_copy(
                msg.at[phase, pl.ds(0, 1)], box.at[pl.ds(slot, 1)],
                r_send.at[phase], r_recv.at[phase], at(*by), MESH_ID,
            ).start()
        drains.append(pltpu.make_async_remote_copy(
            box.at[pl.ds(0, count)], box.at[pl.ds(0, count)],
            r_send.at[phase], r_recv.at[phase], sibling, MESH_ID))
        drains[phase].wait_send()
        if phase == 1:
            finish()
        drains[phase].wait_recv()
        if phase == 0:
            hear(2)
        row = jnp.sum(box[...], axis=0, keepdims=True)

    full = jnp.broadcast_to(row, (8, 128))
    rr, dq, rq, qq = (
        jnp.sum(jnp.where(lane1 // 32 == k, full, 0.0), axis=1, keepdims=True) for k in range(4))
    alpha = rr / dq
    beta = (rr - 2.0 * alpha * rq + alpha * alpha * qq) / rr
    coef[...] = jnp.where(lax.broadcasted_iota(jnp.int32, (8, 128), 0) == 0, alpha, beta)


def apply(solution, residual, direction, slope_il, slope_xl, weights):
    hbm, vmem = pl.BlockSpec(memory_space=pltpu.HBM), pl.BlockSpec(memory_space=pltpu.VMEM)
    block, plane, line = (ROWS, COLS, NT), (COLS, NT), (ROWS, NT)
    dma = pltpu.SemaphoreType.DMA
    operands = (
        pltpu.with_memory_space_constraint(v, pltpu.HBM)
        for v in (solution, residual, direction, slope_il, slope_xl, weights))
    return pl.pallas_call(
        kernel,
        out_shape=(jax.ShapeDtypeStruct(block, F32),) * 4 + (jax.ShapeDtypeStruct((8, 128), F32),),
        in_specs=[hbm] * 6,
        out_specs=(vmem,) * 5,
        scratch_shapes=[
            pltpu.VMEM(shape, F32)
            for shape in (
                block, block, block, block, (ROWS, COLS + 8, NT), block, plane, plane, plane, plane, plane, plane,
                line, line, (2 * ROWS, NT), (2 * ROWS, NT), (2, 8, 128), (32, 128), (16, 128))
        ] + [
            dma((6,)), dma((5,)), dma((5,)), dma((4,)), dma((4,)), dma((2,)), dma((2,)), dma((2,)), dma((2,)),
            pltpu.SemaphoreType.REGULAR((6,))],
        compiler_params=pltpu.CompilerParams(
            collective_id=0, has_side_effects=True, vmem_limit_bytes=24 * 2**20),
    )(*operands)


def update_kernel(sol, res, u, image, coef, new_sol_hbm, new_res_hbm, new_dir_hbm, outs, sems):
    alpha = jnp.broadcast_to(coef[0:1, 0:128], (8, 128))
    beta = jnp.broadcast_to(coef[1:2, 0:128], (8, 128))
    alpha = jnp.concatenate([alpha] * (NT // 128), axis=1)
    beta = jnp.concatenate([beta] * (NT // 128), axis=1)
    copies = []
    for i in range(ROWS):
        def strip(jb, _, i=i):
            rows = pl.ds(pl.multiple_of(jb * 8, 8), 8)
            here = u[i, rows]
            r = res[i, rows] - alpha * image[i, rows]
            outs[0, i, rows] = sol[i, rows] + alpha * here
            outs[1, i, rows] = r
            outs[2, i, rows] = r + beta * here
            return 0
        lax.fori_loop(0, STRIPS, strip, 0, unroll=True)
        for k, target in enumerate((new_sol_hbm, new_res_hbm, new_dir_hbm)):
            copies.append(pltpu.make_async_copy(outs.at[k, i], target.at[i], sems.at[k, i]))
            copies[-1].start()
    for copy in copies:
        copy.wait()


def update(sol, res, u, image, coef):
    hbm, vmem = pl.BlockSpec(memory_space=pl.ANY), pl.BlockSpec(memory_space=pltpu.VMEM)
    block = (ROWS, COLS, NT)
    return pl.pallas_call(
        update_kernel,
        out_shape=(jax.ShapeDtypeStruct(block, F32),) * 3,
        in_specs=[vmem] * 5,
        out_specs=(hbm,) * 3,
        scratch_shapes=[pltpu.VMEM((3,) + block, F32), pltpu.SemaphoreType.DMA((3, ROWS))],
        compiler_params=pltpu.CompilerParams(vmem_limit_bytes=8 * 2**20),
    )(sol, res, u, image, coef)


def body(solution, residual, direction, slope_il, slope_xl, weights):
    return update(*apply(solution, residual, direction, slope_il, slope_xl, weights))


def solution(mesh):
    spec = P("il", "xl", None)
    return jax.shard_map(
        body, mesh=mesh, in_specs=(spec,) * 6, out_specs=(spec,) * 3, check_vma=False)
```
